128 devices in a mesh: dp: 64 (over z, y, x), tensor: 2 (over core).
Axes of the slice: x: 4, y: 4, z: 4, core: 2. Of those that a mesh axis runs over, the one named last changes fastest.
Arguments:
- acts: bfloat16 [32768, 2304], P('dp'), may hold values from -6 to 6
- grad_out: bfloat16 [32768, 4608], P('dp', 'tensor'), may hold values from -0.25 to 0.25
- old_error: bfloat16 [147456, 4608], P('dp', 'tensor'), may hold values from -6 to 6
- old_factor: bfloat16 [32, 4608], P(None, 'tensor'), may hold values from -0.09375 to 0.09375
- piece_order: int32 [8], replicated, may hold values from 0 to 7, each once
Outputs:
- new_error: bfloat16 [147456, 4608], P('dp', 'tensor')
- basis: float32 [2304, 32], replicated
- new_factor: float32 [32, 4608], P(None, 'tensor')
The draws below stay inside these ranges and needn't reach their ends.
Inputs may be any that keep to these rules, and one draw needn't show every extreme that they name: `piece_order`: a permutation of 0 to 7.
All inputs are finite; a program needn't handle non-finite values.
Results may differ from the reference program's by a relative error of at most 0.0049.
Values may be sent and summed in bfloat16 or wider, within the bound.
No kernel may reach another device: no remote copies, remote signals or barrier semaphores. Data moves between devices by JAX's collectives and lax.ppermute only.
A program may use at most 192 MiB of HBM per device.

```python
import jax
import jax.numpy as jnp
from jax import lax

D_WIN = 2304
RANK = 32
GROUPS = 8
TOK_DEV = 512
COLS = 4608
PIECE = 288
N_DP = 64
N_TENSOR = 2


def levels(stream_key, shape, shards, least, largest):
    factor_of = 1.0
    for dim, blocks in shards:
        heights = jax.random.uniform(jax.random.fold_in(jax.random.fold_in(stream_key, 6), dim), (blocks,), jnp.float32, least / len(shards), largest / len(shards))
        factor_of = factor_of * jnp.repeat(jnp.exp(heights), shape[dim] // blocks).reshape((-1,) + (1,) * (len(shape) - 1 - dim))
    return factor_of


def gaussian(stream_key, shape, spread, most, cuts=(), dtype=jnp.bfloat16):
    level = levels(stream_key, shape, cuts, -0.22, 0.18) if cuts else 1.0
    array = jax.random.normal(stream_key, shape, jnp.float32) * spread * level
    return jnp.minimum(jnp.maximum(array, -most), most).astype(dtype)


def setup_inputs(seed: int = 0) -> dict:
    key_list = jax.random.split(jax.random.key(seed), 6)
    return {
        "acts": gaussian(key_list[0], (N_DP * TOK_DEV, D_WIN), 1.0, 6.0, ((0, 64),)),
        "grad_out": gaussian(key_list[1], (N_DP * TOK_DEV, COLS), TOK_DEV ** -0.5, 0.25, ((0, 64), (1, 2))),
        "old_error": gaussian(key_list[2], (N_DP * D_WIN, COLS), 1.0, 6.0, ((0, 64), (1, 2))),
        "old_factor": gaussian(key_list[3], (RANK, COLS), COLS ** -0.5, 0.09375, ((1, 2),)),
        "piece_order": jax.random.permutation(key_list[4], GROUPS).astype(jnp.int32),
    }


def regroup(block, piece_order):
    rows = block.shape[0]
    per_dest = GROUPS // N_TENSOR
    split = block.reshape(rows, N_TENSOR, GROUPS, PIECE)
    picked = jnp.take(split, piece_order, axis=2)
    picked = picked.reshape(rows, N_TENSOR, N_TENSOR, per_dest, PIECE)
    return jnp.transpose(picked, (0, 2, 1, 3, 4)).reshape(rows, COLS)

def reference(acts, grad_out, old_error, old_factor, piece_order):
    error = regroup(old_error, piece_order)
    factor = regroup(old_factor, piece_order)
    acts_rep = acts.reshape(N_DP, TOK_DEV, D_WIN)
    grads_rep = grad_out.reshape(N_DP, TOK_DEV, COLS)
    error_rep = error.reshape(N_DP, D_WIN, COLS)

    def corrected_of(items):
        inputs, cotangent, buffer = items
        grad = lax.dot_general(inputs.astype(jnp.float32), cotangent.astype(jnp.float32), (((0,), (0,)), ((), ())), preferred_element_type=jnp.float32)
        return (grad + buffer.astype(jnp.float32)).astype(jnp.bfloat16)
    corrected = lax.map(corrected_of, (acts_rep, grads_rep, error_rep))

    def add_left(total, matrix):
        term = lax.dot_general(matrix.astype(jnp.float32), factor.astype(jnp.float32), (((1,), (1,)), ((), ())), preferred_element_type=jnp.float32)
        return (total + term, None)
    sums, _ = lax.scan(add_left, jnp.zeros((D_WIN, RANK), jnp.float32), corrected)
    gram = jnp.dot(sums.T, sums, precision=lax.Precision.HIGHEST)
    lower = jnp.linalg.cholesky(gram)
    basis = lax.linalg.triangular_solve(lower, sums, left_side=False, lower=True, transpose_a=True)
    basis_b = basis.astype(jnp.bfloat16)

    def add_right(total, matrix):
        term = lax.dot_general(basis_b.astype(jnp.float32), matrix.astype(jnp.float32), (((0,), (0,)), ((), ())), preferred_element_type=jnp.float32)
        return (total + term, None)
    right_sum, _ = lax.scan(add_right, jnp.zeros((RANK, COLS), jnp.float32), corrected)
    new_factor = right_sum / N_DP
    factor_b = new_factor.astype(jnp.bfloat16)
    approx = jnp.dot(basis_b.astype(jnp.float32), factor_b.astype(jnp.float32), preferred_element_type=jnp.float32)

    def residue(matrix):
        return (matrix.astype(jnp.float32) - approx).astype(jnp.bfloat16)
    new_error = lax.map(residue, corrected).reshape(N_DP * D_WIN, COLS)
    return (new_error, basis, new_factor)
```

```python
import functools

import jax
import jax.numpy as jnp
from jax import lax
from jax.experimental import pallas as pl
from jax.experimental.pallas import tpu as pltpu
from jax.sharding import PartitionSpec as P

BF, F32 = jnp.bfloat16, jnp.float32
ROWS, WIDTH, HALF, RANK, TOK = 2304, 2304, 1152, 32, 512
PIECE, QUARTER = 288, 4
LANES = 128
BLK = 256
HI = lax.Precision.HIGHEST
AXES = ("dp", "tensor")


def dot(a, b, dims, precision=None):
    return lax.dot_general(a, b, (dims, ((), ())), precision=precision, preferred_element_type=F32)


def params(mib=40):
    return pltpu.CompilerParams(vmem_limit_bytes=mib * 2**20)


def vmem(shape, dtype):
    return pltpu.VMEM(shape, dtype)


def in_vmem(x):
    return pltpu.with_memory_space_constraint(x, pltpu.VMEM)


WHOLE = pl.BlockSpec(memory_space=pltpu.VMEM)


def regroup(meta_ref, src_ref, dst_ref, first):
    rows = src_ref.shape[0]
    lane = lax.broadcasted_iota(jnp.int32, (rows, LANES), 1)
    carry = None
    for k in range(QUARTER):
        piece = meta_ref[first + k]
        start = pl.multiple_of(((piece * 9) // 4) * LANES, LANES)
        window = src_ref[:, pl.ds(start, 3 * LANES)].astype(F32)
        shift = 32 * k - 32 * (piece % 4)
        window = pltpu.roll(window, jnp.where(shift < 0, shift + 3 * LANES, shift), 1)
        tile = (PIECE * k) // LANES
        tiles = [window[:, i * LANES : (i + 1) * LANES] for i in range(3)]
        if k:
            tiles[0] = jnp.where(lane < 32 * k, carry, tiles[0])
        carry = tiles[2]
        last = 3 if k == QUARTER - 1 else 2
        for i in range(last):
            dst_ref[:, (tile + i) * LANES : (tile + i + 1) * LANES] = tiles[i].astype(dst_ref.dtype)


def left_kernel(meta_ref, err_ref, fac_ref, left_ref, send_ref, own_ref):
    me = meta_ref[8]
    left_ref[...] = dot(fac_ref[...], err_ref[...], ((1,), (1,)))
    regroup(meta_ref, err_ref, send_ref, (1 - me) * QUARTER)
    regroup(meta_ref, err_ref, own_ref, me * QUARTER)


def left_part(meta, old_error, old_factor):
    grid_spec = pltpu.PrefetchScalarGridSpec(
        num_scalar_prefetch=1,
        grid=(ROWS // BLK,),
        in_specs=[
            pl.BlockSpec((BLK, WIDTH), lambda i, m: (i, 0)),
            pl.BlockSpec((RANK, WIDTH), lambda i, m: (0, 0)),
        ],
        out_specs=[
            pl.BlockSpec((RANK, BLK), lambda i, m: (0, i)),
            pl.BlockSpec((BLK, HALF), lambda i, m: (i, 0)),
            pl.BlockSpec((BLK, HALF), lambda i, m: (i, 0)),
        ],
    )
    return pl.pallas_call(
        left_kernel,
        grid_spec=grid_spec,
        out_shape=[
            jax.ShapeDtypeStruct((RANK, ROWS), F32),
            jax.ShapeDtypeStruct((ROWS, HALF), BF),
            jax.ShapeDtypeStruct((ROWS, HALF), BF),
        ],
        compiler_params=params(),
        cost_estimate=pl.CostEstimate(flops=2 * RANK * ROWS * WIDTH, bytes_accessed=20 * 2**20, transcendentals=0),
        name="left_part",
    )(meta, old_error, old_factor)


def grad_term_kernel(meta_ref, fac_ref, other_ref, left_ref, acts_ref, grad_ref, keep_ref, give_ref, fac_new):
    me = meta_ref[8]
    own_at = pl.multiple_of(me * HALF, LANES)
    other_at = pl.multiple_of((1 - me) * HALF, LANES)
    regroup(meta_ref, fac_ref, fac_new.at[:, pl.ds(own_at, HALF)], me * QUARTER)
    regroup(meta_ref, other_ref, fac_new.at[:, pl.ds(other_at, HALF)], me * QUARTER)
    u = dot(fac_new[...], grad_ref[...], ((1,), (1,)))
    high = u.astype(BF)
    low = (u - high.astype(F32)).astype(BF)
    both = dot(jnp.concatenate([high, low], 0), acts_ref[...], ((1,), (0,)))
    total = left_ref[...] + both[:RANK] + both[RANK:]
    half = RANK // 2
    keep_ref[...] = jnp.where(me == 0, total[:half], total[half:])
    give_ref[...] = jnp.where(me == 0, total[half:], total[:half])


def grad_term(meta, old_factor, other_factor, left, acts, grad_out):
    return pl.pallas_call(
        grad_term_kernel,
        in_specs=[pl.BlockSpec(memory_space=pltpu.SMEM)] + [WHOLE] * 5,
        out_specs=[WHOLE, WHOLE],
        out_shape=[jax.ShapeDtypeStruct((RANK // 2, ROWS), F32)] * 2,
        scratch_shapes=[pltpu.VMEM((RANK, WIDTH), BF)],
        compiler_params=params(),
        name="grad_term",
    )(meta, old_factor, other_factor, left, acts, grad_out)


def grad_kernel(meta_ref, acts_ref, grad_ref, err_ref, out_ref):
    g = dot(acts_ref[...], grad_ref[...], ((0,), (0,)))
    out_ref[...] = (g + err_ref[...].astype(F32)).astype(BF)


def corrected_half(meta, acts, grad_out, err, other):
    def column(i, m):
        return (0, (1 - m[8]) if other else m[8])

    grid_spec = pltpu.PrefetchScalarGridSpec(
        num_scalar_prefetch=1,
        grid=(ROWS // BLK,),
        in_specs=[
            pl.BlockSpec((TOK, BLK), lambda i, m: (0, i)),
            pl.BlockSpec((TOK, HALF), column),
            pl.BlockSpec((BLK, HALF), lambda i, m: (i, 0)),
        ],
        out_specs=pl.BlockSpec((BLK, HALF), lambda i, m: (i, 0)),
    )
    return pl.pallas_call(
        grad_kernel,
        grid_spec=grid_spec,
        out_shape=jax.ShapeDtypeStruct((ROWS, HALF), BF),
        compiler_params=params(),
        cost_estimate=pl.CostEstimate(flops=2 * TOK * ROWS * HALF, bytes_accessed=12 * 2**20, transcendentals=0),
        name="corrected_other" if other else "corrected_own",
    )(meta, acts, grad_out, err)


def right_kernel(meta_ref, keep_ref, took_ref, own_ref, other_ref, basis_ref, basis_b_ref, right_ref):
    me = meta_ref[8]
    keep, took = keep_ref[...], took_ref[...]
    sums = jnp.concatenate(
        [jnp.where(me == 0, keep, took), jnp.where(me == 0, took, keep)], 0
    )
    gram = dot(sums, sums, ((1,), (1,)), HI)
    row = lax.broadcasted_iota(jnp.int32, (RANK, RANK), 0)
    col = lax.broadcasted_iota(jnp.int32, (RANK, RANK), 1)
    work = jnp.concatenate([gram, (row == col).astype(F32)], 1)
    row2 = lax.broadcasted_iota(jnp.int32, (RANK, 2 * RANK), 0)
    for k in range(RANK):
        pivot_row = work[k : k + 1, :]
        scale = lax.rsqrt(pivot_row[:, k : k + 1])
        pivot_row = pivot_row * scale
        column = work[:, k : k + 1] * scale
        work = jnp.where(
            row2 == k, pivot_row, jnp.where(row2 > k, work - column * pivot_row, work)
        )
    inverse = work[:, RANK:]
    basis = dot(inverse, sums, ((1,), (0,)), HI)
    basis_ref[...] = basis
    basis_b = basis.astype(BF)
    basis_b_ref[...] = basis_b
    own_at = pl.multiple_of(me * HALF, LANES)
    other_at = pl.multiple_of((1 - me) * HALF, LANES)
    right_ref[:, pl.ds(own_at, HALF)] = dot(basis_b, own_ref[...], ((1,), (0,))).astype(BF)
    right_ref[:, pl.ds(other_at, HALF)] = dot(basis_b, other_ref[...], ((1,), (0,))).astype(BF)


def right_part(meta, keep, took, own, other):
    return pl.pallas_call(
        right_kernel,
        in_specs=[pl.BlockSpec(memory_space=pltpu.SMEM)] + [WHOLE] * 4,
        out_specs=[WHOLE] * 3,
        out_shape=[
            jax.ShapeDtypeStruct((RANK, ROWS), F32),
            jax.ShapeDtypeStruct((RANK, ROWS), BF),
            jax.ShapeDtypeStruct((RANK, WIDTH), BF),
        ],
        compiler_params=params(),
        name="right_part",
    )(meta, keep, took, own, other)


def residue_kernel(scale, meta_ref, a_ref, b_ref, c_ref, d_ref, basis_b_ref, own_ref, other_ref, err_ref, fac_ref, fac_b):
    i = pl.program_id(0)

    @pl.when(i == 0)
    def _():
        total = (a_ref[...].astype(F32) + b_ref[...].astype(F32)) + (
            c_ref[...].astype(F32) + d_ref[...].astype(F32)
        )
        factor = total * scale
        fac_ref[...] = factor
        fac_b[...] = factor.astype(BF)

    me = meta_ref[8]
    basis_b = basis_b_ref[...]
    for src, who in ((own_ref, me), (other_ref, 1 - me)):
        at = pl.multiple_of(who * HALF, LANES)
        approx = dot(basis_b, fac_b[:, pl.ds(at, HALF)], ((0,), (0,)))
        err_ref[:, pl.ds(at, HALF)] = (src[...].astype(F32) - approx).astype(BF)


def residue(meta, terms, basis_b, own, other, scale):
    def fixed(i, m):
        return (0, 0)

    grid_spec = pltpu.PrefetchScalarGridSpec(
        num_scalar_prefetch=1,
        grid=(ROWS // BLK,),
        in_specs=[pl.BlockSpec((RANK, WIDTH), fixed)] * 4
        + [
            pl.BlockSpec((RANK, BLK), lambda i, m: (0, i)),
            pl.BlockSpec((BLK, HALF), lambda i, m: (i, 0)),
            pl.BlockSpec((BLK, HALF), lambda i, m: (i, 0)),
        ],
        out_specs=[
            pl.BlockSpec((BLK, WIDTH), lambda i, m: (i, 0)),
            pl.BlockSpec((RANK, WIDTH), fixed),
        ],
        scratch_shapes=[pltpu.VMEM((RANK, WIDTH), BF)],
    )
    return pl.pallas_call(
        functools.partial(residue_kernel, scale),
        grid_spec=grid_spec,
        out_shape=[
            jax.ShapeDtypeStruct((ROWS, WIDTH), BF),
            jax.ShapeDtypeStruct((RANK, WIDTH), F32),
        ],
        compiler_params=params(),
        name="residue",
    )(meta, *terms, basis_b, own, other)


def ring_pairs(axes, flip):
    pairs = []
    for index in range(64):
        for core in range(2):
            pairs.append((index * 2 + core, (index ^ (flip << (2 * axes[core]))) * 2 + core))
    return pairs


STAGES = ((0, 1), (1, 2), (2, 0))


def spread(x, axes):
    return [x] + [lax.ppermute(x, AXES, ring_pairs(axes, flip)) for flip in (2, 1, 3)]


def add4(terms):
    a, b, c, d = (t.astype(F32) for t in terms)
    return (a + b) + (c + d)


SWAP = [(0, 1), (1, 0)]


def body(acts, grad_out, old_error, old_factor, piece_order):
    me = lax.axis_index("tensor").astype(jnp.int32)
    meta = jnp.concatenate([piece_order, me[None]])
    other_factor = lax.ppermute(old_factor, "tensor", SWAP)
    left, send, own_err = left_part(meta, old_error, old_factor)
    keep, give = grad_term(meta, old_factor, other_factor, left, acts, grad_out)
    took = lax.ppermute(give, "tensor", SWAP)
    other_err = lax.ppermute(send, "tensor", SWAP)
    part = keep + took
    for axes in STAGES:
        part = add4(spread(part, axes))
    other_part = lax.ppermute(part, "tensor", SWAP)
    own = corrected_half(meta, acts, grad_out, own_err, False)
    other = corrected_half(meta, acts, grad_out, other_err, True)
    basis_t, basis_b, right = right_part(meta, part, other_part, own, other)
    for axes in STAGES[:-1]:
        right = add4(spread(right, axes)).astype(BF)
    terms = spread(right, STAGES[-1])
    new_error, new_factor = residue(meta, terms, basis_b, own, other, 1.0 / lax.axis_size("dp"))
    return (new_error, basis_t.T, new_factor)


def solution(mesh):
    return jax.shard_map(
        body,
        mesh=mesh,
        in_specs=(P("dp", None), P("dp", "tensor"), P("dp", "tensor"), P(None, "tensor"), P()),
        out_specs=(P("dp", "tensor"), P(), P(None, "tensor")),
        check_vma=False,
    )
```

```python
import functools

import jax
import jax.numpy as jnp
from jax import lax
from jax.experimental import pallas as pl
from jax.experimental.pallas import tpu as pltpu
from jax.sharding import PartitionSpec as P

BF, F32 = jnp.bfloat16, jnp.float32
ROWS, WIDTH, HALF, RANK, TOK = 2304, 2304, 1152, 32, 512
PIECE, QUARTER, LANES = 288, 4, 128
BIG, SMALL = 768, 256
HI = lax.Precision.HIGHEST
AXES = ("dp", "tensor")

WHOLE = pl.BlockSpec(memory_space=pltpu.VMEM)
SCALARS = pl.BlockSpec(memory_space=pltpu.SMEM)
FAR = pl.BlockSpec(memory_space=pltpu.HBM)


def dot(a, b, dims, precision=None):
    return lax.dot_general(a, b, (dims, ((), ())), precision=precision, preferred_element_type=F32)


def in_vmem(x):
    return pltpu.with_memory_space_constraint(x, pltpu.VMEM)


def in_hbm(x):
    return pltpu.with_memory_space_constraint(x, pltpu.HBM)


def call(kernel, name, in_specs, outs, scratch=(), mib=16, flops=0, bytes_accessed=0, aliases=None):
    return pl.pallas_call(
        kernel,
        in_specs=in_specs,
        out_specs=[FAR if o.memory_space == pltpu.HBM else WHOLE for o in outs],
        out_shape=outs,
        scratch_shapes=list(scratch),
        compiler_params=pltpu.CompilerParams(vmem_limit_bytes=mib * 2**20),
        cost_estimate=pl.CostEstimate(flops=flops, bytes_accessed=bytes_accessed, transcendentals=0),
        name=name,
        input_output_aliases=aliases or {},
    )


def columns(who):
    return pl.ds(pl.multiple_of(who * HALF, LANES), HALF)


def regroup(order_ref, src_ref, dst_ref, first, rows=None):
    if rows is None:
        rows = pl.ds(0, src_ref.shape[0])
    lane = lax.broadcasted_iota(jnp.int32, (rows.size, LANES), 1)
    carry = None
    for k in range(QUARTER):
        piece = order_ref[first + k]
        start = pl.multiple_of(((piece * 9) // 4) * LANES, LANES)
        window = src_ref[rows, pl.ds(start, 3 * LANES)]
        shift = 32 * k - 32 * (piece % 4)
        window = pltpu.roll(window, jnp.where(shift < 0, shift + 3 * LANES, shift), 1)
        tile = (PIECE * k) // LANES
        tiles = [window[:, i * LANES : (i + 1) * LANES] for i in range(3)]
        if k:
            tiles[0] = jnp.where(lane < 32 * k, carry, tiles[0])
        carry = tiles[2]
        for i in range(3 if k == QUARTER - 1 else 2):
            dst_ref[rows, (tile + i) * LANES : (tile + i + 1) * LANES] = tiles[i]


def rows_at(i, size):
    return pl.ds(pl.multiple_of(i * size, size), size)


def load_kernel(far_order, far_fac, far_err, far_acts, far_grad, left_ref, own_ref, err_ref, acts_ref, grad_ref, fac, order_ref, sems):
    chunks = ROWS // BIG

    def fetch(i):
        rows = rows_at(i, BIG)
        return pltpu.make_async_copy(far_err.at[rows], err_ref.at[rows], sems.at[i])

    others = [
        pltpu.make_async_copy(src, dst, sems.at[chunks + n])
        for n, (src, dst) in enumerate(((far_fac, fac), (far_order, order_ref), (far_grad, grad_ref), (far_acts, acts_ref)))
    ]
    others[0].start()
    others[1].start()
    for i in range(chunks):
        fetch(i).start()
    others[2].start()
    others[3].start()
    me = lax.axis_index("tensor")
    others[0].wait()
    others[1].wait()

    @pl.loop(0, chunks)
    def _(i):
        fetch(i).wait()
        rows = rows_at(i, BIG)
        left_ref[:, rows] = dot(err_ref[rows, :], fac[...], ((1,), (1,))).T
        regroup(order_ref, err_ref, own_ref, me * QUARTER, rows)

    others[2].wait()
    others[3].wait()


def load_part(order, old_factor, old_error, acts, grad_out):
    return call(
        load_kernel,
        "load_part",
        [FAR] * 5,
        [
            pltpu.VMEM((RANK, ROWS), F32),
            pltpu.VMEM((ROWS, HALF), BF),
            pltpu.VMEM((ROWS, WIDTH), BF),
            pltpu.VMEM((TOK, ROWS), BF),
            pltpu.VMEM((TOK, WIDTH), BF),
        ],
        [
            pltpu.VMEM((RANK, WIDTH), BF),
            pltpu.SMEM((2 * QUARTER,), jnp.int32),
            pltpu.SemaphoreType.DMA((ROWS // BIG + 4,)),
        ],
        flops=2 * RANK * ROWS * WIDTH,
        bytes_accessed=2 * ROWS * WIDTH,
    )(in_hbm(order), in_hbm(old_factor), in_hbm(old_error), in_hbm(acts), in_hbm(grad_out))


def term_kernel(order_ref, fac_ref, other_ref, left_ref, acts_ref, grad_ref, keep_ref, give_ref, fac_new, total):
    me = lax.axis_index("tensor")
    regroup(order_ref, fac_ref, fac_new.at[:, columns(me)], me * QUARTER)
    regroup(order_ref, other_ref, fac_new.at[:, columns(1 - me)], me * QUARTER)
    u = dot(fac_new[...], grad_ref[...], ((1,), (1,)))
    high = u.astype(BF)
    low = (u - high.astype(F32)).astype(BF)
    both = dot(jnp.concatenate([high, low], 0), acts_ref[...], ((1,), (0,)))
    total[...] = left_ref[...] + (both[:RANK] + both[RANK:])
    half = RANK // 2
    keep_ref[...] = total[rows_at(me, half), :]
    give_ref[...] = total[rows_at(1 - me, half), :]


def term_part(order, old_factor, other_factor, left, acts, grad_out):
    half = pltpu.VMEM((RANK // 2, ROWS), F32)
    return call(
        term_kernel,
        "term_part",
        [SCALARS] + [WHOLE] * 5,
        [half, half],
        [pltpu.VMEM((RANK, WIDTH), BF), pltpu.VMEM((RANK, ROWS), F32)],
        flops=4 * RANK * ROWS * TOK,
        bytes_accessed=5 * 10**6,
    )(order, old_factor, other_factor, in_vmem(left), in_vmem(acts), in_vmem(grad_out))


def send_kernel(order_ref, after_ref, err_ref, send_ref):
    other = 1 - lax.axis_index("tensor")

    @pl.loop(0, ROWS // BIG)
    def _(i):
        regroup(order_ref, err_ref, send_ref, other * QUARTER, rows_at(i, BIG))


def send_part(order, after, err):
    return call(
        send_kernel,
        "send_part",
        [SCALARS, pl.BlockSpec(memory_space=pl.ANY), WHOLE],
        [pltpu.VMEM((ROWS, HALF), BF)],
        flops=10**9,
        bytes_accessed=4 * 10**6,
    )(order, after, in_vmem(err))[0]


def add_grad(acts_ref, grad_ref, who, err_ref, out_ref):
    @pl.loop(0, ROWS // BIG)
    def _(i):
        rows = pl.ds(pl.multiple_of(i * BIG, BIG), BIG)
        grad = dot(acts_ref[:, rows], grad_ref[:, columns(who)], ((0,), (0,)))
        out_ref[rows, :] = (grad + err_ref[rows, :].astype(F32)).astype(BF)


def half_kernel(other, after_ref, acts_ref, grad_ref, err_ref, out_ref):
    me = lax.axis_index("tensor")
    add_grad(acts_ref, grad_ref, 1 - me if other else me, err_ref, out_ref)


def corrected_half(other, after, acts, grad_out, err):
    return call(
        functools.partial(half_kernel, other),
        "corrected_other" if other else "corrected_own",
        [pl.BlockSpec(memory_space=pl.ANY)] + [WHOLE] * 3,
        [pltpu.VMEM((ROWS, HALF), BF)],
        flops=2 * TOK * ROWS * HALF,
        bytes_accessed=8 * 10**6,
    )(after, in_vmem(acts), in_vmem(grad_out), in_vmem(err))[0]


def right_kernel(keep_ref, took_ref, own_ref, other_ref, basis_ref, basis_b_ref, right_ref):
    me = lax.axis_index("tensor")
    keep, took = keep_ref[...], took_ref[...]
    sums = jnp.concatenate([jnp.where(me == 0, keep, took), jnp.where(me == 0, took, keep)], 0)
    gram = dot(sums, sums, ((1,), (1,)), HI)
    row = lax.broadcasted_iota(jnp.int32, (RANK, RANK), 0)
    col = lax.broadcasted_iota(jnp.int32, (RANK, RANK), 1)
    work = jnp.concatenate([gram, (row == col).astype(F32)], 1)
    row2 = lax.broadcasted_iota(jnp.int32, (RANK, 2 * RANK), 0)
    for k in range(RANK - 1):
        column = jnp.broadcast_to(work[:, k : k + 1], work.shape)
        pivot_row = work[k : k + 1, :] * (1.0 / column[k : k + 1, :])
        work = jnp.where(row2 > k, work - column * pivot_row, work)
    pivots = jnp.sum(jnp.where(row == col, work[:, :RANK], 0.0), 1, keepdims=True)
    inverse = work[:, RANK:] * lax.rsqrt(pivots)
    basis = dot(inverse, sums, ((1,), (0,)), HI)
    basis_ref[...] = basis
    basis_b = basis.astype(BF)
    basis_b_ref[...] = basis_b
    right_ref[:, columns(me)] = dot(basis_b, own_ref[...], ((1,), (0,))).astype(BF)
    right_ref[:, columns(1 - me)] = dot(basis_b, other_ref[...], ((1,), (0,))).astype(BF)


def right_part(keep, took, own, other):
    return call(
        right_kernel,
        "right_part",
        [WHOLE] * 4,
        [pltpu.VMEM((RANK, ROWS), F32), pltpu.VMEM((RANK, ROWS), BF), pltpu.VMEM((RANK, WIDTH), BF)],
        flops=2 * RANK * ROWS * WIDTH,
        bytes_accessed=2 * ROWS * WIDTH,
    )(keep, took, in_vmem(own), in_vmem(other))


STEP = 384


def residue_kernel(scale, a_ref, b_ref, c_ref, d_ref, basis_b_ref, own_ref, other_ref, err_ref, far_ref, fac_ref, fac_b, stage, sems, fac_sem):
    total = (a_ref[...].astype(F32) + b_ref[...].astype(F32)) + (c_ref[...].astype(F32) + d_ref[...].astype(F32))
    factor = total * scale
    fac_ref[...] = factor
    fac_copy = pltpu.make_async_copy(fac_ref, far_ref, fac_sem)
    fac_copy.start()
    fac_b[...] = factor.astype(BF)
    me = lax.axis_index("tensor")

    def store(i):
        rows = pl.ds(pl.multiple_of(i * STEP, STEP), STEP)
        return pltpu.make_async_copy(stage.at[rows], err_ref.at[rows], sems.at[i])

    @pl.loop(0, ROWS // STEP)
    def _(i):
        rows = pl.ds(pl.multiple_of(i * STEP, STEP), STEP)
        for src, who in ((own_ref, me), (other_ref, 1 - me)):
            approx = dot(basis_b_ref[:, rows], fac_b[:, columns(who)], ((0,), (0,)))
            stage[rows, columns(who)] = (src[rows, :].astype(F32) - approx).astype(BF)
        store(i).start()

    @pl.loop(0, ROWS // STEP)
    def _(i):
        store(i).wait()

    fac_copy.wait()


def residue(terms, basis_b, own, other, scale):
    return call(
        functools.partial(residue_kernel, scale),
        "residue",
        [WHOLE] * 7,
        [pltpu.HBM((ROWS, WIDTH), BF), pltpu.HBM((RANK, WIDTH), F32)],
        [
            pltpu.VMEM((RANK, WIDTH), F32),
            pltpu.VMEM((RANK, WIDTH), BF),
            pltpu.VMEM((ROWS, WIDTH), BF),
            pltpu.SemaphoreType.DMA((ROWS // STEP,)),
            pltpu.SemaphoreType.DMA,
        ],
        mib=24,
        flops=2 * RANK * ROWS * WIDTH,
        bytes_accessed=2 * ROWS * WIDTH,
    )(*terms, basis_b, in_vmem(own), in_vmem(other))


def ring_pairs(axes, flip):
    pairs = []
    for index in range(64):
        for core in range(2):
            pairs.append((index * 2 + core, (index ^ (flip << (2 * axes[core]))) * 2 + core))
    return pairs


STAGES = ((0, 1), (1, 2), (2, 0))
SWAP = [(0, 1), (1, 0)]


def spread(x, axes):
    return [x] + [lax.ppermute(x, AXES, ring_pairs(axes, flip)) for flip in (2, 1, 3)]


def add4(terms):
    a, b, c, d = (t.astype(F32) for t in terms)
    return (a + b) + (c + d)


def add_kernel(a_ref, b_ref, c_ref, d_ref, work_ref, sum_ref, work_out_ref):
    sum_ref[...] = (a_ref[...] + b_ref[...]) + (c_ref[...] + d_ref[...])


def add_after(terms, work):
    return call(
        add_kernel,
        "add_terms",
        [WHOLE] * 4 + [pl.BlockSpec(memory_space=pl.ANY)],
        [pltpu.VMEM(terms[0].shape, F32), pltpu.VMEM(work.shape, work.dtype)],
        bytes_accessed=10**6,
        aliases={4: 1},
    )(*terms, in_vmem(work))


def body(acts, grad_out, old_error, old_factor, piece_order):
    other_factor = lax.ppermute(old_factor, "tensor", SWAP)
    left, own_err, err, acts, grad_out = load_part(piece_order, old_factor, old_error, acts, grad_out)
    keep, give = term_part(piece_order, old_factor, other_factor, left, acts, grad_out)
    part = keep + lax.ppermute(give, "tensor", SWAP)
    terms = spread(part, STAGES[0])
    part, send = add_after(terms, send_part(piece_order, part, err))
    other_err = lax.ppermute(send, "tensor", SWAP)
    terms = spread(part, STAGES[1])
    part, own = add_after(terms, corrected_half(False, part, acts, grad_out, own_err))
    terms = spread(part, STAGES[2])
    part, other = add_after(terms, corrected_half(True, part, acts, grad_out, other_err))
    basis_t, basis_b, right = right_part(part, lax.ppermute(part, "tensor", SWAP), own, other)
    for axes in STAGES[:-1]:
        right = add4(spread(right, axes)).astype(BF)
    terms = spread(right, STAGES[-1])
    new_error, new_factor = residue(terms, basis_b, own, other, 1.0 / lax.axis_size("dp"))
    return (new_error, basis_t.T, new_factor)


def solution(mesh):
    return jax.shard_map(
        body,
        mesh=mesh,
        in_specs=(P("dp", None), P("dp", "tensor"), P("dp", "tensor"), P(None, "tensor"), P()),
        out_specs=(P("dp", "tensor"), P(), P(None, "tensor")),
        check_vma=False,
    )
```

```python
import functools

import jax
import jax.numpy as jnp
from jax import lax
from jax.experimental import pallas as pl
from jax.experimental.pallas import tpu as pltpu
from jax.sharding import PartitionSpec as P

BF, F32 = jnp.bfloat16, jnp.float32
ROWS, WIDTH, HALF, RANK, TOK = 2304, 2304, 1152, 32, 512
PIECE, QUARTER, LANES = 288, 4, 128
BIG, SMALL = 768, 256
HI = lax.Precision.HIGHEST
AXES = ("dp", "tensor")

WHOLE = pl.BlockSpec(memory_space=pltpu.VMEM)
SCALARS = pl.BlockSpec(memory_space=pltpu.SMEM)
FAR = pl.BlockSpec(memory_space=pltpu.HBM)


def dot(a, b, dims, precision=None):
    return lax.dot_general(a, b, (dims, ((), ())), precision=precision, preferred_element_type=F32)


def in_vmem(x):
    return pltpu.with_memory_space_constraint(x, pltpu.VMEM)


def in_hbm(x):
    return pltpu.with_memory_space_constraint(x, pltpu.HBM)


def call(kernel, name, in_specs, outs, scratch=(), mib=16, flops=0, bytes_accessed=0, aliases=None):
    return pl.pallas_call(
        kernel,
        in_specs=in_specs,
        out_specs=[FAR if o.memory_space == pltpu.HBM else WHOLE for o in outs],
        out_shape=outs,
        scratch_shapes=list(scratch),
        compiler_params=pltpu.CompilerParams(vmem_limit_bytes=mib * 2**20),
        cost_estimate=pl.CostEstimate(flops=flops, bytes_accessed=bytes_accessed, transcendentals=0),
        name=name,
        input_output_aliases=aliases or {},
    )


def columns(who):
    return pl.ds(pl.multiple_of(who * HALF, LANES), HALF)


def regroup(order_ref, src_ref, dst_ref, first, rows=None):
    if rows is None:
        rows = pl.ds(0, src_ref.shape[0])
    lane = lax.broadcasted_iota(jnp.int32, (rows.size, LANES), 1)
    carry = None
    for k in range(QUARTER):
        piece = order_ref[first + k]
        start = pl.multiple_of(((piece * 9) // 4) * LANES, LANES)
        window = src_ref[rows, pl.ds(start, 3 * LANES)]
        shift = 32 * k - 32 * (piece % 4)
        window = pltpu.roll(window, jnp.where(shift < 0, shift + 3 * LANES, shift), 1)
        tile = (PIECE * k) // LANES
        tiles = [window[:, i * LANES : (i + 1) * LANES] for i in range(3)]
        if k:
            tiles[0] = jnp.where(lane < 32 * k, carry, tiles[0])
        carry = tiles[2]
        for i in range(3 if k == QUARTER - 1 else 2):
            dst_ref[rows, (tile + i) * LANES : (tile + i + 1) * LANES] = tiles[i]


def rows_at(i, size):
    return pl.ds(pl.multiple_of(i * size, size), size)


def load_kernel(far_order, far_fac, far_err, far_acts, far_grad, left_ref, own_ref, err_ref, acts_ref, grad_ref, fac, order_ref, sems):
    chunks = ROWS // BIG

    def fetch(i):
        rows = rows_at(i, BIG)
        return pltpu.make_async_copy(far_err.at[rows], err_ref.at[rows], sems.at[i])

    others = [
        pltpu.make_async_copy(src, dst, sems.at[chunks + n])
        for n, (src, dst) in enumerate(((far_fac, fac), (far_order, order_ref), (far_grad, grad_ref), (far_acts, acts_ref)))
    ]
    others[0].start()
    others[1].start()
    for i in range(chunks):
        fetch(i).start()
    others[2].start()
    others[3].start()
    me = lax.axis_index("tensor")
    others[0].wait()
    others[1].wait()

    @pl.loop(0, chunks)
    def _(i):
        fetch(i).wait()
        rows = rows_at(i, BIG)
        left_ref[:, rows] = dot(err_ref[rows, :], fac[...], ((1,), (1,))).T
        regroup(order_ref, err_ref, own_ref, me * QUARTER, rows)

    others[2].wait()
    others[3].wait()


def load_part(order, old_factor, old_error, acts, grad_out):
    return call(
        load_kernel,
        "load_part",
        [FAR] * 5,
        [
            pltpu.VMEM((RANK, ROWS), F32),
            pltpu.VMEM((ROWS, HALF), BF),
            pltpu.VMEM((ROWS, WIDTH), BF),
            pltpu.VMEM((TOK, ROWS), BF),
            pltpu.VMEM((TOK, WIDTH), BF),
        ],
        [
            pltpu.VMEM((RANK, WIDTH), BF),
            pltpu.SMEM((2 * QUARTER,), jnp.int32),
            pltpu.SemaphoreType.DMA((ROWS // BIG + 4,)),
        ],
        flops=2 * RANK * ROWS * WIDTH,
        bytes_accessed=2 * ROWS * WIDTH,
    )(in_hbm(order), in_hbm(old_factor), in_hbm(old_error), in_hbm(acts), in_hbm(grad_out))


def term_kernel(order_ref, fac_ref, other_ref, left_ref, acts_ref, grad_ref, keep_ref, give_ref, fac_new, total):
    me = lax.axis_index("tensor")
    regroup(order_ref, fac_ref, fac_new.at[:, columns(me)], me * QUARTER)
    regroup(order_ref, other_ref, fac_new.at[:, columns(1 - me)], me * QUARTER)
    u = dot(fac_new[...], grad_ref[...], ((1,), (1,)))
    high = u.astype(BF)
    low = (u - high.astype(F32)).astype(BF)
    both = dot(jnp.concatenate([high, low], 0), acts_ref[...], ((1,), (0,)))
    total[...] = left_ref[...] + (both[:RANK] + both[RANK:])
    half = RANK // 2
    keep_ref[...] = total[rows_at(me, half), :]
    give_ref[...] = total[rows_at(1 - me, half), :]


def term_part(order, old_factor, other_factor, left, acts, grad_out):
    half = pltpu.VMEM((RANK // 2, ROWS), F32)
    return call(
        term_kernel,
        "term_part",
        [SCALARS] + [WHOLE] * 5,
        [half, half],
        [pltpu.VMEM((RANK, WIDTH), BF), pltpu.VMEM((RANK, ROWS), F32)],
        flops=4 * RANK * ROWS * TOK,
        bytes_accessed=5 * 10**6,
    )(order, old_factor, other_factor, in_vmem(left), in_vmem(acts), in_vmem(grad_out))


def send_kernel(order_ref, after_ref, err_ref, send_ref):
    other = 1 - lax.axis_index("tensor")

    @pl.loop(0, ROWS // BIG)
    def _(i):
        regroup(order_ref, err_ref, send_ref, other * QUARTER, rows_at(i, BIG))


def send_part(order, after, err):
    return call(
        send_kernel,
        "send_part",
        [SCALARS, pl.BlockSpec(memory_space=pl.ANY), WHOLE],
        [pltpu.VMEM((ROWS, HALF), BF)],
        flops=10**9,
        bytes_accessed=4 * 10**6,
    )(order, after, in_vmem(err))[0]


def add_grad(acts_ref, grad_ref, who, err_ref, out_ref):
    @pl.loop(0, ROWS // BIG)
    def _(i):
        rows = pl.ds(pl.multiple_of(i * BIG, BIG), BIG)
        grad = dot(acts_ref[:, rows], grad_ref[:, columns(who)], ((0,), (0,)))
        out_ref[rows, :] = (grad + err_ref[rows, :].astype(F32)).astype(BF)


def half_kernel(other, after_ref, acts_ref, grad_ref, err_ref, out_ref):
    me = lax.axis_index("tensor")
    add_grad(acts_ref, grad_ref, 1 - me if other else me, err_ref, out_ref)


def corrected_half(other, after, acts, grad_out, err):
    return call(
        functools.partial(half_kernel, other),
        "corrected_other" if other else "corrected_own",
        [pl.BlockSpec(memory_space=pl.ANY)] + [WHOLE] * 3,
        [pltpu.VMEM((ROWS, HALF), BF)],
        flops=2 * TOK * ROWS * HALF,
        bytes_accessed=8 * 10**6,
    )(after, in_vmem(acts), in_vmem(grad_out), in_vmem(err))[0]


def split3(x):
    terms = []
    for _ in range(3):
        terms.append(x.astype(BF))
        x = x - terms[-1].astype(F32)
    return jnp.concatenate(terms, 0)


def inverse_factor(gram):
    row = lax.broadcasted_iota(jnp.int32, (RANK, RANK), 0)
    col = lax.broadcasted_iota(jnp.int32, (RANK, RANK), 1)
    work = jnp.concatenate([gram, (row == col).astype(F32)], 1)
    wide = lax.broadcasted_iota(jnp.int32, work.shape, 0)
    for k in range(0, RANK, 2):
        first = jnp.broadcast_to(work[:, k : k + 1], work.shape)
        second = jnp.broadcast_to(work[:, k + 1 : k + 2], work.shape)
        row0 = work[k : k + 1, :]
        inv0 = 1.0 / first[k : k + 1, :]
        ratio = first[k + 1 : k + 2, :] * inv0
        row1 = work[k + 1 : k + 2, :] - ratio * row0
        pivot1 = second[k + 1 : k + 2, :] - ratio * first[k + 1 : k + 2, :]
        second = second - first * ratio
        below = work - first * (row0 * inv0) - second * (row1 * (1.0 / pivot1))
        work = jnp.where(wide > k + 1, below, jnp.where(wide == k + 1, row1, work))
    pivots = jnp.sum(jnp.where(row == col, work[:, :RANK], 0.0), 1, keepdims=True)
    return work[:, RANK:] * lax.rsqrt(pivots)


def right_kernel(keep_ref, took_ref, own_ref, other_ref, basis_ref, basis_b_ref, right_ref):
    me = lax.axis_index("tensor")
    keep, took = keep_ref[...], took_ref[...]
    sums = jnp.concatenate([jnp.where(me == 0, keep, took), jnp.where(me == 0, took, keep)], 0)
    gram = dot(sums, sums, ((1,), (1,)), HI)
    terms = split3(sums)
    halves = []
    for ref in (own_ref, other_ref):
        x = dot(terms, ref[...], ((1,), (0,)))
        halves.append(x[:RANK] + (x[RANK : 2 * RANK] + x[2 * RANK :]))
    inverse = inverse_factor(gram)
    basis = dot(inverse, sums, ((1,), (0,)), HI)
    basis_ref[...] = basis
    basis_b_ref[...] = basis.astype(BF)
    for half, who in zip(halves, (me, 1 - me)):
        right_ref[:, columns(who)] = dot(inverse, half, ((1,), (0,)), HI).astype(BF)


def right_part(keep, took, own, other):
    return call(
        right_kernel,
        "right_part",
        [WHOLE] * 4,
        [pltpu.VMEM((RANK, ROWS), F32), pltpu.VMEM((RANK, ROWS), BF), pltpu.VMEM((RANK, WIDTH), BF)],
        flops=2 * RANK * ROWS * WIDTH,
        bytes_accessed=2 * ROWS * WIDTH,
    )(keep, took, in_vmem(own), in_vmem(other))


STEP = 192


def residue_kernel(scale, a_ref, b_ref, c_ref, d_ref, basis_b_ref, own_ref, other_ref, err_ref, far_ref, fac_ref, fac_b, stage, sems, fac_sem):
    total = (a_ref[...].astype(F32) + b_ref[...].astype(F32)) + (c_ref[...].astype(F32) + d_ref[...].astype(F32))
    factor = total * scale
    fac_ref[...] = factor
    fac_copy = pltpu.make_async_copy(fac_ref, far_ref, fac_sem)
    fac_copy.start()
    me = lax.axis_index("tensor")
    fac_b[:, :HALF] = fac_ref[:, columns(me)].astype(BF)
    fac_b[:, HALF:] = fac_ref[:, columns(1 - me)].astype(BF)

    def store(i):
        rows = pl.ds(i * STEP, STEP)
        return pltpu.make_async_copy(stage.at[rows], err_ref.at[rows], sems.at[i])

    for i in range(ROWS // STEP):
        rows = pl.ds(i * STEP, STEP)
        for n, (src, who) in enumerate(((own_ref, me), (other_ref, 1 - me))):
            approx = dot(basis_b_ref[:, rows], fac_b[:, n * HALF : (n + 1) * HALF], ((0,), (0,)))
            stage[rows, columns(who)] = (src[rows, :].astype(F32) - approx).astype(BF)
        store(i).start()
    for i in range(ROWS // STEP):
        store(i).wait()
    fac_copy.wait()


def residue(terms, basis_b, own, other, scale):
    return call(
        functools.partial(residue_kernel, scale),
        "residue",
        [WHOLE] * 7,
        [pltpu.HBM((ROWS, WIDTH), BF), pltpu.HBM((RANK, WIDTH), F32)],
        [
            pltpu.VMEM((RANK, WIDTH), F32),
            pltpu.VMEM((RANK, WIDTH), BF),
            pltpu.VMEM((ROWS, WIDTH), BF),
            pltpu.SemaphoreType.DMA((ROWS // STEP,)),
            pltpu.SemaphoreType.DMA,
        ],
        mib=24,
        flops=2 * RANK * ROWS * WIDTH,
        bytes_accessed=2 * ROWS * WIDTH,
    )(*terms, basis_b, in_vmem(own), in_vmem(other))


def ring_pairs(axes, flip):
    pairs = []
    for index in range(64):
        for core in range(2):
            pairs.append((index * 2 + core, (index ^ (flip << (2 * axes[core]))) * 2 + core))
    return pairs


STAGES = ((0, 1), (1, 2), (2, 0))
SWAP = [(0, 1), (1, 0)]


def spread(x, axes):
    return [x] + [lax.ppermute(x, AXES, ring_pairs(axes, flip)) for flip in (2, 1, 3)]


def add4(terms):
    a, b, c, d = (t.astype(F32) for t in terms)
    return (a + b) + (c + d)


def add_kernel(a_ref, b_ref, c_ref, d_ref, work_ref, sum_ref, work_out_ref):
    sum_ref[...] = (a_ref[...] + b_ref[...]) + (c_ref[...] + d_ref[...])


def add_after(terms, work):
    return call(
        add_kernel,
        "add_terms",
        [WHOLE] * 4 + [pl.BlockSpec(memory_space=pl.ANY)],
        [pltpu.VMEM(terms[0].shape, F32), pltpu.VMEM(work.shape, work.dtype)],
        bytes_accessed=10**6,
        aliases={4: 1},
    )(*terms, in_vmem(work))


def body(acts, grad_out, old_error, old_factor, piece_order):
    other_factor = lax.ppermute(old_factor, "tensor", SWAP)
    left, own_err, err, acts, grad_out = load_part(piece_order, old_factor, old_error, acts, grad_out)
    keep, give = term_part(piece_order, old_factor, other_factor, left, acts, grad_out)
    part = keep + lax.ppermute(give, "tensor", SWAP)
    terms = spread(part, STAGES[0])
    part, send = add_after(terms, send_part(piece_order, part, err))
    other_err = lax.ppermute(send, "tensor", SWAP)
    terms = spread(part, STAGES[1])
    part, own = add_after(terms, corrected_half(False, part, acts, grad_out, own_err))
    terms = spread(part, STAGES[2])
    part, other = add_after(terms, corrected_half(True, part, acts, grad_out, other_err))
    basis_t, basis_b, right = right_part(part, lax.ppermute(part, "tensor", SWAP), own, other)
    for axes in STAGES[:-1]:
        right = add4(spread(right, axes)).astype(BF)
    terms = spread(right, STAGES[-1])
    new_error, new_factor = residue(terms, basis_b, own, other, 1.0 / lax.axis_size("dp"))
    return (new_error, basis_t.T, new_factor)


def solution(mesh):
    return jax.shard_map(
        body,
        mesh=mesh,
        in_specs=(P("dp", None), P("dp", "tensor"), P("dp", "tensor"), P(None, "tensor"), P()),
        out_specs=(P("dp", "tensor"), P(), P(None, "tensor")),
        check_vma=False,
    )
```

```python
import functools

import jax
import jax.numpy as jnp
from jax import lax
from jax.experimental import pallas as pl
from jax.experimental.pallas import tpu as pltpu
from jax.sharding import PartitionSpec as P

BF, F32 = jnp.bfloat16, jnp.float32
ROWS, WIDTH, HALF, RANK, TOK = 2304, 2304, 1152, 32, 512
PIECE, QUARTER, LANES = 288, 4, 128
BIG, SMALL = 768, 256
HI = lax.Precision.HIGHEST
AXES = ("dp", "tensor")

WHOLE = pl.BlockSpec(memory_space=pltpu.VMEM)
SCALARS = pl.BlockSpec(memory_space=pltpu.SMEM)
FAR = pl.BlockSpec(memory_space=pltpu.HBM)


def dot(a, b, dims, precision=None):
    return lax.dot_general(a, b, (dims, ((), ())), precision=precision, preferred_element_type=F32)


def in_vmem(x):
    return pltpu.with_memory_space_constraint(x, pltpu.VMEM)


def in_hbm(x):
    return pltpu.with_memory_space_constraint(x, pltpu.HBM)


def call(kernel, name, in_specs, outs, scratch=(), mib=16, flops=0, bytes_accessed=0, aliases=None):
    return pl.pallas_call(
        kernel,
        in_specs=in_specs,
        out_specs=[FAR if o.memory_space == pltpu.HBM else WHOLE for o in outs],
        out_shape=outs,
        scratch_shapes=list(scratch),
        compiler_params=pltpu.CompilerParams(vmem_limit_bytes=mib * 2**20),
        cost_estimate=pl.CostEstimate(flops=flops, bytes_accessed=bytes_accessed, transcendentals=0),
        name=name,
        input_output_aliases=aliases or {},
    )


def columns(who):
    return pl.ds(pl.multiple_of(who * HALF, LANES), HALF)


def regroup(order_ref, src_ref, dst_ref, first, rows=None):
    if rows is None:
        rows = pl.ds(0, src_ref.shape[0])
    lane = lax.broadcasted_iota(jnp.int32, (rows.size, LANES), 1)
    carry = None
    for k in range(QUARTER):
        piece = order_ref[first + k]
        start = pl.multiple_of(((piece * 9) // 4) * LANES, LANES)
        window = src_ref[rows, pl.ds(start, 3 * LANES)]
        shift = 32 * k - 32 * (piece % 4)
        window = pltpu.roll(window, jnp.where(shift < 0, shift + 3 * LANES, shift), 1)
        tile = (PIECE * k) // LANES
        tiles = [window[:, i * LANES : (i + 1) * LANES] for i in range(3)]
        if k:
            tiles[0] = jnp.where(lane < 32 * k, carry, tiles[0])
        carry = tiles[2]
        for i in range(3 if k == QUARTER - 1 else 2):
            dst_ref[rows, (tile + i) * LANES : (tile + i + 1) * LANES] = tiles[i]


def rows_at(i, size):
    return pl.ds(pl.multiple_of(i * size, size), size)


def load_kernel(far_order, far_fac, far_err, far_acts, far_grad, left_ref, own_ref, err_ref, acts_ref, grad_ref, fac, order_ref, sems):
    chunks = ROWS // BIG

    def fetch(i):
        rows = rows_at(i, BIG)
        return pltpu.make_async_copy(far_err.at[rows], err_ref.at[rows], sems.at[i])

    others = [
        pltpu.make_async_copy(src, dst, sems.at[chunks + n])
        for n, (src, dst) in enumerate(((far_fac, fac), (far_order, order_ref), (far_grad, grad_ref), (far_acts, acts_ref)))
    ]
    others[0].start()
    others[1].start()
    for i in range(chunks):
        fetch(i).start()
    others[2].start()
    others[3].start()
    me = lax.axis_index("tensor")
    others[0].wait()
    others[1].wait()

    @pl.loop(0, chunks)
    def _(i):
        fetch(i).wait()
        rows = rows_at(i, BIG)
        left_ref[:, rows] = dot(err_ref[rows, :], fac[...], ((1,), (1,))).T
        regroup(order_ref, err_ref, own_ref, me * QUARTER, rows)

    others[2].wait()
    others[3].wait()


def load_part(order, old_factor, old_error, acts, grad_out):
    return call(
        load_kernel,
        "load_part",
        [FAR] * 5,
        [
            pltpu.VMEM((RANK, ROWS), F32),
            pltpu.VMEM((ROWS, HALF), BF),
            pltpu.VMEM((ROWS, WIDTH), BF),
            pltpu.VMEM((TOK, ROWS), BF),
            pltpu.VMEM((TOK, WIDTH), BF),
        ],
        [
            pltpu.VMEM((RANK, WIDTH), BF),
            pltpu.SMEM((2 * QUARTER,), jnp.int32),
            pltpu.SemaphoreType.DMA((ROWS // BIG + 4,)),
        ],
        flops=2 * RANK * ROWS * WIDTH,
        bytes_accessed=2 * ROWS * WIDTH,
    )(in_hbm(order), in_hbm(old_factor), in_hbm(old_error), in_hbm(acts), in_hbm(grad_out))


def term_kernel(order_ref, fac_ref, other_ref, left_ref, acts_ref, grad_ref, keep_ref, give_ref, fac_new, total):
    me = lax.axis_index("tensor")
    regroup(order_ref, fac_ref, fac_new.at[:, columns(me)], me * QUARTER)
    regroup(order_ref, other_ref, fac_new.at[:, columns(1 - me)], me * QUARTER)
    u = dot(fac_new[...], grad_ref[...], ((1,), (1,)))
    high = u.astype(BF)
    low = (u - high.astype(F32)).astype(BF)
    both = dot(jnp.concatenate([high, low], 0), acts_ref[...], ((1,), (0,)))
    total[...] = left_ref[...] + (both[:RANK] + both[RANK:])
    half = RANK // 2
    keep_ref[...] = total[rows_at(me, half), :]
    give_ref[...] = total[rows_at(1 - me, half), :]


def term_part(order, old_factor, other_factor, left, acts, grad_out):
    half = pltpu.VMEM((RANK // 2, ROWS), F32)
    return call(
        term_kernel,
        "term_part",
        [SCALARS] + [WHOLE] * 5,
        [half, half],
        [pltpu.VMEM((RANK, WIDTH), BF), pltpu.VMEM((RANK, ROWS), F32)],
        flops=4 * RANK * ROWS * TOK,
        bytes_accessed=5 * 10**6,
    )(order, old_factor, other_factor, in_vmem(left), in_vmem(acts), in_vmem(grad_out))


def send_kernel(order_ref, after_ref, err_ref, send_ref):
    other = 1 - lax.axis_index("tensor")

    @pl.loop(0, ROWS // BIG)
    def _(i):
        regroup(order_ref, err_ref, send_ref, other * QUARTER, rows_at(i, BIG))


def send_part(order, after, err):
    return call(
        send_kernel,
        "send_part",
        [SCALARS, pl.BlockSpec(memory_space=pl.ANY), WHOLE],
        [pltpu.VMEM((ROWS, HALF), BF)],
        flops=10**9,
        bytes_accessed=4 * 10**6,
    )(order, after, in_vmem(err))[0]


def add_grad(acts_ref, grad_ref, who, err_ref, out_ref):
    @pl.loop(0, ROWS // BIG)
    def _(i):
        rows = pl.ds(pl.multiple_of(i * BIG, BIG), BIG)
        grad = dot(acts_ref[:, rows], grad_ref[:, columns(who)], ((0,), (0,)))
        out_ref[rows, :] = (grad + err_ref[rows, :].astype(F32)).astype(BF)


def half_kernel(other, after_ref, acts_ref, grad_ref, err_ref, out_ref):
    me = lax.axis_index("tensor")
    add_grad(acts_ref, grad_ref, 1 - me if other else me, err_ref, out_ref)


def corrected_half(other, after, acts, grad_out, err):
    return call(
        functools.partial(half_kernel, other),
        "corrected_other" if other else "corrected_own",
        [pl.BlockSpec(memory_space=pl.ANY)] + [WHOLE] * 3,
        [pltpu.VMEM((ROWS, HALF), BF)],
        flops=2 * TOK * ROWS * HALF,
        bytes_accessed=8 * 10**6,
    )(after, in_vmem(acts), in_vmem(grad_out), in_vmem(err))[0]


def split3(x):
    terms = []
    for _ in range(3):
        terms.append(x.astype(BF))
        x = x - terms[-1].astype(F32)
    return jnp.concatenate(terms, 0)


def inverse_factor(gram):
    row = lax.broadcasted_iota(jnp.int32, (RANK, RANK), 0)
    col = lax.broadcasted_iota(jnp.int32, (RANK, RANK), 1)
    work = jnp.concatenate([gram, (row == col).astype(F32)], 1)
    wide = lax.broadcasted_iota(jnp.int32, work.shape, 0)
    for k in range(0, RANK, 2):
        first = jnp.broadcast_to(work[:, k : k + 1], work.shape)
        second = jnp.broadcast_to(work[:, k + 1 : k + 2], work.shape)
        row0 = work[k : k + 1, :]
        inv0 = 1.0 / first[k : k + 1, :]
        ratio = first[k + 1 : k + 2, :] * inv0
        row1 = work[k + 1 : k + 2, :] - ratio * row0
        pivot1 = second[k + 1 : k + 2, :] - ratio * first[k + 1 : k + 2, :]
        second = second - first * ratio
        below = work - first * (row0 * inv0) - second * (row1 * (1.0 / pivot1))
        work = jnp.where(wide > k + 1, below, jnp.where(wide == k + 1, row1, work))
    pivots = jnp.sum(jnp.where(row == col, work[:, :RANK], 0.0), 1, keepdims=True)
    return work[:, RANK:] * lax.rsqrt(pivots)


def right_kernel(keep_ref, took_ref, own_ref, other_ref, basis_ref, basis_b_ref, right_ref):
    me = lax.axis_index("tensor")
    keep, took = keep_ref[...], took_ref[...]
    sums = jnp.concatenate([jnp.where(me == 0, keep, took), jnp.where(me == 0, took, keep)], 0)
    gram = dot(sums, sums, ((1,), (1,)), HI)
    terms = split3(sums)
    halves = []
    for ref in (own_ref, other_ref):
        x = dot(terms, ref[...], ((1,), (0,)))
        halves.append(x[:RANK] + (x[RANK : 2 * RANK] + x[2 * RANK :]))
    inverse = inverse_factor(gram)
    basis = dot(inverse, sums, ((1,), (0,)), HI)
    basis_ref[...] = basis
    basis_b_ref[...] = basis.astype(BF)
    for half, who in zip(halves, (me, 1 - me)):
        right_ref[:, columns(who)] = dot(inverse, half, ((1,), (0,)), HI).astype(BF)


def right_part(keep, took, own, other):
    return call(
        right_kernel,
        "right_part",
        [WHOLE] * 4,
        [pltpu.VMEM((RANK, ROWS), F32), pltpu.VMEM((RANK, ROWS), BF), pltpu.VMEM((RANK, WIDTH), BF)],
        flops=2 * RANK * ROWS * WIDTH,
        bytes_accessed=2 * ROWS * WIDTH,
    )(keep, took, in_vmem(own), in_vmem(other))


STEP = 192


def residue_kernel(scale, a_ref, b_ref, c_ref, d_ref, basis_b_ref, own_ref, other_ref, err_ref, far_ref, fac_ref, fac_b, stage, sems, fac_sem):
    total = (a_ref[...].astype(F32) + b_ref[...].astype(F32)) + (c_ref[...].astype(F32) + d_ref[...].astype(F32))
    factor = total * scale
    fac_ref[...] = factor
    fac_copy = pltpu.make_async_copy(fac_ref, far_ref, fac_sem)
    fac_copy.start()
    me = lax.axis_index("tensor")
    fac_b[:, :HALF] = fac_ref[:, columns(me)].astype(BF)
    fac_b[:, HALF:] = fac_ref[:, columns(1 - me)].astype(BF)

    def store(i):
        rows = pl.ds(i * STEP, STEP)
        return pltpu.make_async_copy(stage.at[rows], err_ref.at[rows], sems.at[i])

    for i in range(ROWS // STEP):
        rows = pl.ds(i * STEP, STEP)
        for n, (src, who) in enumerate(((own_ref, me), (other_ref, 1 - me))):
            approx = dot(basis_b_ref[:, rows], fac_b[:, n * HALF : (n + 1) * HALF], ((0,), (0,)))
            stage[rows, columns(who)] = (src[rows, :].astype(F32) - approx).astype(BF)
        store(i).start()
    for i in range(ROWS // STEP):
        store(i).wait()
    fac_copy.wait()


def residue(terms, basis_b, own, other, scale):
    return call(
        functools.partial(residue_kernel, scale),
        "residue",
        [WHOLE] * 7,
        [pltpu.HBM((ROWS, WIDTH), BF), pltpu.HBM((RANK, WIDTH), F32)],
        [
            pltpu.VMEM((RANK, WIDTH), F32),
            pltpu.VMEM((RANK, WIDTH), BF),
            pltpu.VMEM((ROWS, WIDTH), BF),
            pltpu.SemaphoreType.DMA((ROWS // STEP,)),
            pltpu.SemaphoreType.DMA,
        ],
        mib=24,
        flops=2 * RANK * ROWS * WIDTH,
        bytes_accessed=2 * ROWS * WIDTH,
    )(*terms, basis_b, in_vmem(own), in_vmem(other))


def ring_pairs(axes, flip, cross):
    pairs = []
    for index in range(64):
        for core in range(2):
            there = index ^ (flip << (2 * axes[core]))
            pairs.append((index * 2 + core, there * 2 + (core ^ cross)))
    return pairs


FLIPS = (1, 3, 2)
STAGES = ((0, 1), (1, 2), (2, 0))
SWAP = [(0, 1), (1, 0)]


def stages(crosses):
    moved = 0
    for axes, cross in zip(STAGES, crosses):
        yield (axes[::-1] if moved else axes), cross
        moved ^= cross


def spread(x, stage):
    axes, cross = stage
    terms = [lax.ppermute(x, AXES, ring_pairs(axes, flip, cross)) for flip in FLIPS]
    return [lax.ppermute(x, "tensor", SWAP) if cross else x] + terms


def add4(terms):
    a, b, c, d = (t.astype(F32) for t in terms)
    return (a + b) + (c + d)


def add_kernel(a_ref, b_ref, c_ref, d_ref, work_ref, sum_ref, work_out_ref):
    sum_ref[...] = (a_ref[...] + b_ref[...]) + (c_ref[...] + d_ref[...])


def add_after(terms, work):
    return call(
        add_kernel,
        "add_terms",
        [WHOLE] * 4 + [pl.BlockSpec(memory_space=pl.ANY)],
        [pltpu.VMEM(terms[0].shape, F32), pltpu.VMEM(work.shape, work.dtype)],
        bytes_accessed=10**6,
        aliases={4: 1},
    )(*terms, in_vmem(work))


def body(acts, grad_out, old_error, old_factor, piece_order):
    other_factor = lax.ppermute(old_factor, "tensor", SWAP)
    left, own_err, err, acts, grad_out = load_part(piece_order, old_factor, old_error, acts, grad_out)
    keep, give = term_part(piece_order, old_factor, other_factor, left, acts, grad_out)
    part = keep + lax.ppermute(give, "tensor", SWAP)
    first, second, third = stages((1, 0, 1))
    terms = spread(part, first)
    part, send = add_after(terms, send_part(piece_order, part, err))
    other_err = lax.ppermute(send, "tensor", SWAP)
    terms = spread(part, second)
    part, own = add_after(terms, corrected_half(False, part, acts, grad_out, own_err))
    terms = spread(part, third)
    part, other = add_after(terms, corrected_half(True, part, acts, grad_out, other_err))
    basis_t, basis_b, right = right_part(part, lax.ppermute(part, "tensor", SWAP), own, other)
    first, second, third = stages((1, 1, 0))
    for stage in (first, second):
        right = add4(spread(right, stage)).astype(BF)
    terms = spread(right, third)
    new_error, new_factor = residue(terms, basis_b, own, other, 1.0 / lax.axis_size("dp"))
    return (new_error, basis_t.T, new_factor)


def solution(mesh):
    return jax.shard_map(
        body,
        mesh=mesh,
        in_specs=(P("dp", None), P("dp", "tensor"), P("dp", "tensor"), P(None, "tensor"), P()),
        out_specs=(P("dp", "tensor"), P(), P(None, "tensor")),
        check_vma=False,
    )
```

```python
import functools

import jax
import jax.numpy as jnp
from jax import lax
from jax.experimental import pallas as pl
from jax.experimental.pallas import tpu as pltpu
from jax.sharding import PartitionSpec as P

BF, F32 = jnp.bfloat16, jnp.float32
ROWS, WIDTH, HALF, RANK, TOK = 2304, 2304, 1152, 32, 512
PIECE, QUARTER, LANES = 288, 4, 128
BIG, SMALL = 768, 256
HI = lax.Precision.HIGHEST
AXES = ("dp", "tensor")

WHOLE = pl.BlockSpec(memory_space=pltpu.VMEM)
SCALARS = pl.BlockSpec(memory_space=pltpu.SMEM)
FAR = pl.BlockSpec(memory_space=pltpu.HBM)


def dot(a, b, dims, precision=None):
    return lax.dot_general(a, b, (dims, ((), ())), precision=precision, preferred_element_type=F32)


def in_vmem(x):
    return pltpu.with_memory_space_constraint(x, pltpu.VMEM)


def in_hbm(x):
    return pltpu.with_memory_space_constraint(x, pltpu.HBM)


def call(kernel, name, in_specs, outs, scratch=(), mib=16, flops=0, bytes_accessed=0, aliases=None):
    return pl.pallas_call(
        kernel,
        in_specs=in_specs,
        out_specs=[FAR if o.memory_space == pltpu.HBM else WHOLE for o in outs],
        out_shape=outs,
        scratch_shapes=list(scratch),
        compiler_params=pltpu.CompilerParams(vmem_limit_bytes=mib * 2**20),
        cost_estimate=pl.CostEstimate(flops=flops, bytes_accessed=bytes_accessed, transcendentals=0),
        name=name,
        input_output_aliases=aliases or {},
    )


def columns(who):
    return pl.ds(pl.multiple_of(who * HALF, LANES), HALF)


def regroup(order_ref, src_ref, dst_ref, first, rows=None):
    if rows is None:
        rows = pl.ds(0, src_ref.shape[0])
    lane = lax.broadcasted_iota(jnp.int32, (rows.size, LANES), 1)
    carry = None
    for k in range(QUARTER):
        piece = order_ref[first + k]
        start = pl.multiple_of(((piece * 9) // 4) * LANES, LANES)
        window = src_ref[rows, pl.ds(start, 3 * LANES)]
        shift = 32 * k - 32 * (piece % 4)
        window = pltpu.roll(window, jnp.where(shift < 0, shift + 3 * LANES, shift), 1)
        tile = (PIECE * k) // LANES
        tiles = [window[:, i * LANES : (i + 1) * LANES] for i in range(3)]
        if k:
            tiles[0] = jnp.where(lane < 32 * k, carry, tiles[0])
        carry = tiles[2]
        for i in range(3 if k == QUARTER - 1 else 2):
            dst_ref[rows, (tile + i) * LANES : (tile + i + 1) * LANES] = tiles[i]


def rows_at(i, size):
    return pl.ds(pl.multiple_of(i * size, size), size)


def load_kernel(far_order, far_fac, far_err, far_acts, far_grad, left_ref, own_ref, err_ref, acts_ref, grad_ref, fac, order_ref, sems):
    chunks = ROWS // BIG

    def fetch(i):
        rows = rows_at(i, BIG)
        return pltpu.make_async_copy(far_err.at[rows], err_ref.at[rows], sems.at[i])

    others = [
        pltpu.make_async_copy(src, dst, sems.at[chunks + n])
        for n, (src, dst) in enumerate(((far_fac, fac), (far_order, order_ref), (far_grad, grad_ref), (far_acts, acts_ref)))
    ]
    others[0].start()
    others[1].start()
    for i in range(chunks):
        fetch(i).start()
    others[2].start()
    others[3].start()
    me = lax.axis_index("tensor")
    others[0].wait()
    others[1].wait()

    @pl.loop(0, chunks)
    def _(i):
        fetch(i).wait()
        rows = rows_at(i, BIG)
        left_ref[:, rows] = dot(err_ref[rows, :], fac[...], ((1,), (1,))).T
        regroup(order_ref, err_ref, own_ref, me * QUARTER, rows)

    others[2].wait()
    others[3].wait()


def load_part(order, old_factor, old_error, acts, grad_out):
    return call(
        load_kernel,
        "load_part",
        [FAR] * 5,
        [
            pltpu.VMEM((RANK, ROWS), F32),
            pltpu.VMEM((ROWS, HALF), BF),
            pltpu.VMEM((ROWS, WIDTH), BF),
            pltpu.VMEM((TOK, ROWS), BF),
            pltpu.VMEM((TOK, WIDTH), BF),
        ],
        [
            pltpu.VMEM((RANK, WIDTH), BF),
            pltpu.SMEM((2 * QUARTER,), jnp.int32),
            pltpu.SemaphoreType.DMA((ROWS // BIG + 4,)),
        ],
        flops=2 * RANK * ROWS * WIDTH,
        bytes_accessed=2 * ROWS * WIDTH,
    )(in_hbm(order), in_hbm(old_factor), in_hbm(old_error), in_hbm(acts), in_hbm(grad_out))


def term_kernel(order_ref, fac_ref, other_ref, left_ref, acts_ref, grad_ref, keep_ref, give_ref, fac_new, total):
    me = lax.axis_index("tensor")
    regroup(order_ref, fac_ref, fac_new.at[:, columns(me)], me * QUARTER)
    regroup(order_ref, other_ref, fac_new.at[:, columns(1 - me)], me * QUARTER)
    u = dot(fac_new[...], grad_ref[...], ((1,), (1,)))
    high = u.astype(BF)
    low = (u - high.astype(F32)).astype(BF)
    both = dot(jnp.concatenate([high, low], 0), acts_ref[...], ((1,), (0,)))
    total[...] = left_ref[...] + (both[:RANK] + both[RANK:])
    half = RANK // 2
    keep_ref[...] = total[rows_at(me, half), :]
    give_ref[...] = total[rows_at(1 - me, half), :]


def term_part(order, old_factor, other_factor, left, acts, grad_out):
    half = pltpu.VMEM((RANK // 2, ROWS), F32)
    return call(
        term_kernel,
        "term_part",
        [SCALARS] + [WHOLE] * 5,
        [half, half],
        [pltpu.VMEM((RANK, WIDTH), BF), pltpu.VMEM((RANK, ROWS), F32)],
        flops=4 * RANK * ROWS * TOK,
        bytes_accessed=5 * 10**6,
    )(order, old_factor, other_factor, in_vmem(left), in_vmem(acts), in_vmem(grad_out))


def send_kernel(order_ref, after_ref, err_ref, send_ref):
    other = 1 - lax.axis_index("tensor")

    @pl.loop(0, ROWS // BIG)
    def _(i):
        regroup(order_ref, err_ref, send_ref, other * QUARTER, rows_at(i, BIG))


def send_part(order, after, err):
    return call(
        send_kernel,
        "send_part",
        [SCALARS, pl.BlockSpec(memory_space=pl.ANY), WHOLE],
        [pltpu.VMEM((ROWS, HALF), BF)],
        flops=10**9,
        bytes_accessed=4 * 10**6,
    )(order, after, in_vmem(err))[0]


def add_grad(acts_ref, grad_ref, who, err_ref, out_ref):
    @pl.loop(0, ROWS // BIG)
    def _(i):
        rows = pl.ds(pl.multiple_of(i * BIG, BIG), BIG)
        grad = dot(acts_ref[:, rows], grad_ref[:, columns(who)], ((0,), (0,)))
        out_ref[rows, :] = (grad + err_ref[rows, :].astype(F32)).astype(BF)


def half_kernel(other, after_ref, acts_ref, grad_ref, err_ref, out_ref):
    me = lax.axis_index("tensor")
    add_grad(acts_ref, grad_ref, 1 - me if other else me, err_ref, out_ref)


def corrected_half(other, after, acts, grad_out, err):
    return call(
        functools.partial(half_kernel, other),
        "corrected_other" if other else "corrected_own",
        [pl.BlockSpec(memory_space=pl.ANY)] + [WHOLE] * 3,
        [pltpu.VMEM((ROWS, HALF), BF)],
        flops=2 * TOK * ROWS * HALF,
        bytes_accessed=8 * 10**6,
    )(after, in_vmem(acts), in_vmem(grad_out), in_vmem(err))[0]


def split3(x):
    terms = []
    for _ in range(3):
        terms.append(x.astype(BF))
        x = x - terms[-1].astype(F32)
    return jnp.concatenate(terms, 0)


def inverse_factor(gram):
    row = lax.broadcasted_iota(jnp.int32, (RANK, RANK), 0)
    col = lax.broadcasted_iota(jnp.int32, (RANK, RANK), 1)
    work = jnp.concatenate([gram, (row == col).astype(F32)], 1)
    wide = lax.broadcasted_iota(jnp.int32, work.shape, 0)
    for k in range(0, RANK, 2):
        first = jnp.broadcast_to(work[:, k : k + 1], work.shape)
        second = jnp.broadcast_to(work[:, k + 1 : k + 2], work.shape)
        row0 = work[k : k + 1, :]
        inv0 = 1.0 / first[k : k + 1, :]
        ratio = first[k + 1 : k + 2, :] * inv0
        row1 = work[k + 1 : k + 2, :] - ratio * row0
        pivot1 = second[k + 1 : k + 2, :] - ratio * first[k + 1 : k + 2, :]
        second = second - first * ratio
        below = work - first * (row0 * inv0) - second * (row1 * (1.0 / pivot1))
        work = jnp.where(wide > k + 1, below, jnp.where(wide == k + 1, row1, work))
    pivots = jnp.sum(jnp.where(row == col, work[:, :RANK], 0.0), 1, keepdims=True)
    return work[:, RANK:] * lax.rsqrt(pivots)


def dot3(terms, b):
    n = terms.shape[0] // 3
    x = dot(terms, b, ((1,), (0,)))
    return x[:n] + (x[n : 2 * n] + x[2 * n :])


def dot6(a, b):
    n = a.shape[0]
    terms = split3(a)
    parts = []
    for drop in range(3):
        part = b.astype(BF)
        b = b - part.astype(F32)
        x = dot(terms[: (3 - drop) * n], part, ((1,), (0,)))
        parts.append([x[i * n : (i + 1) * n] for i in range(3 - drop)])
    (x11, x21, x31), (x12, x22), (x13,) = parts
    return x11 + ((x21 + x12) + (x31 + (x22 + x13)))


def right_kernel(keep_ref, took_ref, own_ref, other_ref, inverse_ref, sums_ref, right_ref):
    me = lax.axis_index("tensor")
    keep, took = keep_ref[...], took_ref[...]
    sums = jnp.concatenate([jnp.where(me == 0, keep, took), jnp.where(me == 0, took, keep)], 0)
    sums_ref[...] = sums
    terms = split3(sums)
    pairs = dot(terms, terms, ((1,), (1,)))
    blocks = [[pairs[i * RANK : (i + 1) * RANK, j * RANK : (j + 1) * RANK] for j in range(3)] for i in range(3)]
    gram = blocks[0][0] + ((blocks[0][1] + blocks[1][0]) + (blocks[1][1] + (blocks[0][2] + blocks[2][0])))
    halves = [dot3(terms, ref[...]) for ref in (own_ref, other_ref)]
    inverse = inverse_factor(gram)
    inverse_ref[...] = inverse
    for half, who in zip(halves, (me, 1 - me)):
        right_ref[:, columns(who)] = dot6(inverse, half).astype(BF)


def right_part(keep, took, own, other):
    return call(
        right_kernel,
        "right_part",
        [WHOLE] * 4,
        [pltpu.VMEM((RANK, RANK), F32), pltpu.VMEM((RANK, ROWS), F32), pltpu.VMEM((RANK, WIDTH), BF)],
        flops=2 * RANK * ROWS * WIDTH,
        bytes_accessed=2 * ROWS * WIDTH,
    )(keep, took, in_vmem(own), in_vmem(other))


def basis_kernel(inverse_ref, sums_ref, basis_ref, basis_b_ref):
    basis = dot(inverse_ref[...], sums_ref[...], ((1,), (0,)), HI)
    basis_ref[...] = basis
    basis_b_ref[...] = basis.astype(BF)


def basis_part(inverse, sums):
    return call(
        basis_kernel,
        "basis_part",
        [WHOLE] * 2,
        [pltpu.VMEM((RANK, ROWS), F32), pltpu.VMEM((RANK, ROWS), BF)],
        flops=12 * RANK * RANK * ROWS,
        bytes_accessed=10**6,
    )(in_vmem(inverse), in_vmem(sums))


STEP = 192


def residue_kernel(scale, a_ref, b_ref, c_ref, d_ref, basis_b_ref, own_ref, other_ref, err_ref, far_ref, fac_ref, fac_b, stage, sems, fac_sem):
    total = (a_ref[...].astype(F32) + b_ref[...].astype(F32)) + (c_ref[...].astype(F32) + d_ref[...].astype(F32))
    factor = total * scale
    fac_ref[...] = factor
    fac_copy = pltpu.make_async_copy(fac_ref, far_ref, fac_sem)
    fac_copy.start()
    me = lax.axis_index("tensor")
    fac_b[:, :HALF] = fac_ref[:, columns(me)].astype(BF)
    fac_b[:, HALF:] = fac_ref[:, columns(1 - me)].astype(BF)

    def store(i):
        rows = pl.ds(i * STEP, STEP)
        return pltpu.make_async_copy(stage.at[rows], err_ref.at[rows], sems.at[i])

    for i in range(ROWS // STEP):
        rows = pl.ds(i * STEP, STEP)
        for n, (src, who) in enumerate(((own_ref, me), (other_ref, 1 - me))):
            approx = dot(basis_b_ref[:, rows], fac_b[:, n * HALF : (n + 1) * HALF], ((0,), (0,)))
            stage[rows, columns(who)] = (src[rows, :].astype(F32) - approx).astype(BF)
        store(i).start()
    for i in range(ROWS // STEP):
        store(i).wait()
    fac_copy.wait()


def residue(terms, basis_b, own, other, scale):
    return call(
        functools.partial(residue_kernel, scale),
        "residue",
        [WHOLE] * 7,
        [pltpu.HBM((ROWS, WIDTH), BF), pltpu.HBM((RANK, WIDTH), F32)],
        [
            pltpu.VMEM((RANK, WIDTH), F32),
            pltpu.VMEM((RANK, WIDTH), BF),
            pltpu.VMEM((ROWS, WIDTH), BF),
            pltpu.SemaphoreType.DMA((ROWS // STEP,)),
            pltpu.SemaphoreType.DMA,
        ],
        mib=24,
        flops=2 * RANK * ROWS * WIDTH,
        bytes_accessed=2 * ROWS * WIDTH,
    )(*terms, basis_b, in_vmem(own), in_vmem(other))


def ring_pairs(axes, flip, cross):
    pairs = []
    for index in range(64):
        for core in range(2):
            there = index ^ (flip << (2 * axes[core]))
            pairs.append((index * 2 + core, there * 2 + (core ^ cross)))
    return pairs


FLIPS = (1, 3, 2)
STAGES = ((0, 1), (1, 2), (2, 0))
SWAP = [(0, 1), (1, 0)]


def stages(crosses):
    moved = 0
    for axes, cross in zip(STAGES, crosses):
        yield (axes[::-1] if moved else axes), cross
        moved ^= cross


def spread(x, stage):
    axes, cross = stage
    terms = [lax.ppermute(x, AXES, ring_pairs(axes, flip, cross)) for flip in FLIPS]
    return [lax.ppermute(x, "tensor", SWAP) if cross else x] + terms


def add4(terms):
    a, b, c, d = (t.astype(F32) for t in terms)
    return (a + b) + (c + d)


def add_kernel(a_ref, b_ref, c_ref, d_ref, work_ref, sum_ref, work_out_ref):
    sum_ref[...] = (a_ref[...] + b_ref[...]) + (c_ref[...] + d_ref[...])


def add_after(terms, work):
    return call(
        add_kernel,
        "add_terms",
        [WHOLE] * 4 + [pl.BlockSpec(memory_space=pl.ANY)],
        [pltpu.VMEM(terms[0].shape, F32), pltpu.VMEM(work.shape, work.dtype)],
        bytes_accessed=10**6,
        aliases={4: 1},
    )(*terms, in_vmem(work))


def body(acts, grad_out, old_error, old_factor, piece_order):
    other_factor = lax.ppermute(old_factor, "tensor", SWAP)
    left, own_err, err, acts, grad_out = load_part(piece_order, old_factor, old_error, acts, grad_out)
    keep, give = term_part(piece_order, old_factor, other_factor, left, acts, grad_out)
    part = keep + lax.ppermute(give, "tensor", SWAP)
    first, second, third = stages((1, 0, 1))
    terms = spread(part, first)
    part, send = add_after(terms, send_part(piece_order, part, err))
    other_err = lax.ppermute(send, "tensor", SWAP)
    terms = spread(part, second)
    part, own = add_after(terms, corrected_half(False, part, acts, grad_out, own_err))
    terms = spread(part, third)
    part, other = add_after(terms, corrected_half(True, part, acts, grad_out, other_err))
    inverse, sums, right = right_part(part, lax.ppermute(part, "tensor", SWAP), own, other)
    basis_t, basis_b = basis_part(inverse, sums)
    first, second, third = stages((1, 1, 0))
    for stage in (first, second):
        right = add4(spread(right, stage)).astype(BF)
    terms = spread(right, third)
    new_error, new_factor = residue(terms, basis_b, own, other, 1.0 / lax.axis_size("dp"))
    return (new_error, basis_t.T, new_factor)


def solution(mesh):
    return jax.shard_map(
        body,
        mesh=mesh,
        in_specs=(P("dp", None), P("dp", "tensor"), P("dp", "tensor"), P(None, "tensor"), P()),
        out_specs=(P("dp", "tensor"), P(), P(None, "tensor")),
        check_vma=False,
    )
```

```python
import functools

import jax
import jax.numpy as jnp
from jax import lax
from jax.experimental import pallas as pl
from jax.experimental.pallas import tpu as pltpu
from jax.sharding import PartitionSpec as P

BF, F32 = jnp.bfloat16, jnp.float32
ROWS, WIDTH, HALF, RANK, TOK = 2304, 2304, 1152, 32, 512
PIECE, QUARTER, LANES = 288, 4, 128
BIG, SMALL = 768, 256
HI = lax.Precision.HIGHEST
AXES = ("dp", "tensor")

WHOLE = pl.BlockSpec(memory_space=pltpu.VMEM)
SCALARS = pl.BlockSpec(memory_space=pltpu.SMEM)
FAR = pl.BlockSpec(memory_space=pltpu.HBM)


def dot(a, b, dims, precision=None):
    return lax.dot_general(a, b, (dims, ((), ())), precision=precision, preferred_element_type=F32)


def in_vmem(x):
    return pltpu.with_memory_space_constraint(x, pltpu.VMEM)


def in_hbm(x):
    return pltpu.with_memory_space_constraint(x, pltpu.HBM)


def call(kernel, name, in_specs, outs, scratch=(), mib=16, flops=0, bytes_accessed=0, aliases=None):
    return pl.pallas_call(
        kernel,
        in_specs=in_specs,
        out_specs=[FAR if o.memory_space == pltpu.HBM else WHOLE for o in outs],
        out_shape=outs,
        scratch_shapes=list(scratch),
        compiler_params=pltpu.CompilerParams(vmem_limit_bytes=mib * 2**20),
        cost_estimate=pl.CostEstimate(flops=flops, bytes_accessed=bytes_accessed, transcendentals=0),
        name=name,
        input_output_aliases=aliases or {},
    )


def columns(who):
    return pl.ds(pl.multiple_of(who * HALF, LANES), HALF)


def regroup(order_ref, src_ref, dst_ref, first, rows=None):
    if rows is None:
        rows = pl.ds(0, src_ref.shape[0])
    lane = lax.broadcasted_iota(jnp.int32, (rows.size, LANES), 1)
    carry = None
    for k in range(QUARTER):
        piece = order_ref[first + k]
        start = pl.multiple_of(((piece * 9) // 4) * LANES, LANES)
        window = src_ref[rows, pl.ds(start, 3 * LANES)]
        shift = 32 * k - 32 * (piece % 4)
        window = pltpu.roll(window, jnp.where(shift < 0, shift + 3 * LANES, shift), 1)
        tile = (PIECE * k) // LANES
        tiles = [window[:, i * LANES : (i + 1) * LANES] for i in range(3)]
        if k:
            tiles[0] = jnp.where(lane < 32 * k, carry, tiles[0])
        carry = tiles[2]
        for i in range(3 if k == QUARTER - 1 else 2):
            dst_ref[rows, (tile + i) * LANES : (tile + i + 1) * LANES] = tiles[i]


def rows_at(i, size):
    return pl.ds(pl.multiple_of(i * size, size), size)


def load_kernel(far_order, far_fac, far_err, far_acts, far_grad, left_ref, own_ref, err_ref, acts_ref, grad_ref, fac, order_ref, sems):
    chunks = ROWS // BIG

    def fetch(i):
        rows = rows_at(i, BIG)
        return pltpu.make_async_copy(far_err.at[rows], err_ref.at[rows], sems.at[i])

    others = [
        pltpu.make_async_copy(src, dst, sems.at[chunks + n])
        for n, (src, dst) in enumerate(((far_fac, fac), (far_order, order_ref), (far_grad, grad_ref), (far_acts, acts_ref)))
    ]
    others[0].start()
    others[1].start()
    for i in range(chunks):
        fetch(i).start()
    others[2].start()
    others[3].start()
    me = lax.axis_index("tensor")
    others[0].wait()
    others[1].wait()

    @pl.loop(0, chunks)
    def _(i):
        fetch(i).wait()
        rows = rows_at(i, BIG)
        left_ref[:, rows] = dot(err_ref[rows, :], fac[...], ((1,), (1,))).T
        regroup(order_ref, err_ref, own_ref, me * QUARTER, rows)

    others[2].wait()
    others[3].wait()


def load_part(order, old_factor, old_error, acts, grad_out):
    return call(
        load_kernel,
        "load_part",
        [FAR] * 5,
        [
            pltpu.VMEM((RANK, ROWS), F32),
            pltpu.VMEM((ROWS, HALF), BF),
            pltpu.VMEM((ROWS, WIDTH), BF),
            pltpu.VMEM((TOK, ROWS), BF),
            pltpu.VMEM((TOK, WIDTH), BF),
        ],
        [
            pltpu.VMEM((RANK, WIDTH), BF),
            pltpu.SMEM((2 * QUARTER,), jnp.int32),
            pltpu.SemaphoreType.DMA((ROWS // BIG + 4,)),
        ],
        flops=2 * RANK * ROWS * WIDTH,
        bytes_accessed=2 * ROWS * WIDTH,
    )(in_hbm(order), in_hbm(old_factor), in_hbm(old_error), in_hbm(acts), in_hbm(grad_out))


def term_kernel(order_ref, fac_ref, other_ref, left_ref, acts_ref, grad_ref, keep_ref, give_ref, fac_new, total):
    me = lax.axis_index("tensor")
    regroup(order_ref, fac_ref, fac_new.at[:, columns(me)], me * QUARTER)
    regroup(order_ref, other_ref, fac_new.at[:, columns(1 - me)], me * QUARTER)
    u = dot(fac_new[...], grad_ref[...], ((1,), (1,)))
    high = u.astype(BF)
    low = (u - high.astype(F32)).astype(BF)
    both = dot(jnp.concatenate([high, low], 0), acts_ref[...], ((1,), (0,)))
    total[...] = left_ref[...] + (both[:RANK] + both[RANK:])
    half = RANK // 2
    keep_ref[...] = total[rows_at(me, half), :]
    give_ref[...] = total[rows_at(1 - me, half), :]


def term_part(order, old_factor, other_factor, left, acts, grad_out):
    half = pltpu.VMEM((RANK // 2, ROWS), F32)
    return call(
        term_kernel,
        "term_part",
        [SCALARS] + [WHOLE] * 5,
        [half, half],
        [pltpu.VMEM((RANK, WIDTH), BF), pltpu.VMEM((RANK, ROWS), F32)],
        flops=4 * RANK * ROWS * TOK,
        bytes_accessed=5 * 10**6,
    )(order, old_factor, other_factor, in_vmem(left), in_vmem(acts), in_vmem(grad_out))


def send_kernel(order_ref, after_ref, err_ref, send_ref):
    other = 1 - lax.axis_index("tensor")

    @pl.loop(0, ROWS // BIG)
    def _(i):
        regroup(order_ref, err_ref, send_ref, other * QUARTER, rows_at(i, BIG))


def send_part(order, after, err):
    return call(
        send_kernel,
        "send_part",
        [SCALARS, pl.BlockSpec(memory_space=pl.ANY), WHOLE],
        [pltpu.VMEM((ROWS, HALF), BF)],
        flops=10**9,
        bytes_accessed=4 * 10**6,
    )(order, after, in_vmem(err))[0]


def add_grad(acts_ref, grad_ref, who, err_ref, out_ref):
    @pl.loop(0, ROWS // BIG)
    def _(i):
        rows = pl.ds(pl.multiple_of(i * BIG, BIG), BIG)
        grad = dot(acts_ref[:, rows], grad_ref[:, columns(who)], ((0,), (0,)))
        out_ref[rows, :] = (grad + err_ref[rows, :].astype(F32)).astype(BF)


def half_kernel(other, after_ref, acts_ref, grad_ref, err_ref, out_ref):
    me = lax.axis_index("tensor")
    add_grad(acts_ref, grad_ref, 1 - me if other else me, err_ref, out_ref)


def corrected_half(other, after, acts, grad_out, err):
    return call(
        functools.partial(half_kernel, other),
        "corrected_other" if other else "corrected_own",
        [pl.BlockSpec(memory_space=pl.ANY)] + [WHOLE] * 3,
        [pltpu.VMEM((ROWS, HALF), BF)],
        flops=2 * TOK * ROWS * HALF,
        bytes_accessed=8 * 10**6,
    )(after, in_vmem(acts), in_vmem(grad_out), in_vmem(err))[0]


def split3(x):
    terms = []
    for _ in range(3):
        terms.append(x.astype(BF))
        x = x - terms[-1].astype(F32)
    return jnp.concatenate(terms, 0)


def inverse_factor(gram):
    row = lax.broadcasted_iota(jnp.int32, (RANK, RANK), 0)
    col = lax.broadcasted_iota(jnp.int32, (RANK, RANK), 1)
    work = jnp.concatenate([gram, (row == col).astype(F32)], 1)
    wide = lax.broadcasted_iota(jnp.int32, work.shape, 0)
    for k in range(0, RANK, 2):
        first = jnp.broadcast_to(work[:, k : k + 1], work.shape)
        second = jnp.broadcast_to(work[:, k + 1 : k + 2], work.shape)
        row0 = work[k : k + 1, :]
        inv0 = 1.0 / first[k : k + 1, :]
        ratio = first[k + 1 : k + 2, :] * inv0
        row1 = work[k + 1 : k + 2, :] - ratio * row0
        pivot1 = second[k + 1 : k + 2, :] - ratio * first[k + 1 : k + 2, :]
        second = second - first * ratio
        below = work - first * (row0 * inv0) - second * (row1 * (1.0 / pivot1))
        work = jnp.where(wide > k + 1, below, jnp.where(wide == k + 1, row1, work))
    pivots = jnp.sum(jnp.where(row == col, work[:, :RANK], 0.0), 1, keepdims=True)
    return work[:, RANK:] * lax.rsqrt(pivots)


def dot3(terms, b):
    n = terms.shape[0] // 3
    x = dot(terms, b, ((1,), (0,)))
    return x[:n] + (x[n : 2 * n] + x[2 * n :])


def dot6(a, b):
    n = a.shape[0]
    terms = split3(a)
    parts = []
    for drop in range(3):
        part = b.astype(BF)
        b = b - part.astype(F32)
        x = dot(terms[: (3 - drop) * n], part, ((1,), (0,)))
        parts.append([x[i * n : (i + 1) * n] for i in range(3 - drop)])
    (x11, x21, x31), (x12, x22), (x13,) = parts
    return x11 + ((x21 + x12) + (x31 + (x22 + x13)))


def right_kernel(keep_ref, took_ref, own_ref, other_ref, inverse_ref, sums_ref, right_ref):
    me = lax.axis_index("tensor")
    keep, took = keep_ref[...], took_ref[...]
    sums = jnp.concatenate([jnp.where(me == 0, keep, took), jnp.where(me == 0, took, keep)], 0)
    sums_ref[...] = sums
    terms = split3(sums)
    pairs = dot(terms, terms, ((1,), (1,)))
    blocks = [[pairs[i * RANK : (i + 1) * RANK, j * RANK : (j + 1) * RANK] for j in range(3)] for i in range(3)]
    gram = blocks[0][0] + ((blocks[0][1] + blocks[1][0]) + (blocks[1][1] + (blocks[0][2] + blocks[2][0])))
    halves = [dot3(terms, ref[...]) for ref in (own_ref, other_ref)]
    inverse = inverse_factor(gram)
    inverse_ref[...] = inverse
    for half, who in zip(halves, (me, 1 - me)):
        right_ref[:, columns(who)] = dot6(inverse, half).astype(BF)


def right_part(keep, took, own, other):
    return call(
        right_kernel,
        "right_part",
        [WHOLE] * 4,
        [pltpu.VMEM((RANK, RANK), F32), pltpu.VMEM((RANK, ROWS), F32), pltpu.VMEM((RANK, WIDTH), BF)],
        flops=2 * RANK * ROWS * WIDTH,
        bytes_accessed=2 * ROWS * WIDTH,
    )(keep, took, in_vmem(own), in_vmem(other))


def basis_kernel(inverse_ref, sums_ref, basis_ref, basis_b_ref):
    basis = dot(inverse_ref[...], sums_ref[...], ((1,), (0,)), HI)
    basis_ref[...] = basis
    basis_b_ref[...] = basis.astype(BF)


def basis_part(inverse, sums):
    return call(
        basis_kernel,
        "basis_part",
        [WHOLE] * 2,
        [pltpu.VMEM((RANK, ROWS), F32), pltpu.VMEM((RANK, ROWS), BF)],
        flops=12 * RANK * RANK * ROWS,
        bytes_accessed=10**6,
    )(in_vmem(inverse), in_vmem(sums))


STEP = 192


def residue_kernel(scale, a_ref, b_ref, c_ref, d_ref, basis_b_ref, own_ref, other_ref, err_ref, far_ref, fac_ref, fac_b, stage, sems, fac_sem):
    total = (a_ref[...].astype(F32) + b_ref[...].astype(F32)) + (c_ref[...].astype(F32) + d_ref[...].astype(F32))
    factor = total * scale
    fac_ref[...] = factor
    fac_copy = pltpu.make_async_copy(fac_ref, far_ref, fac_sem)
    fac_copy.start()
    me = lax.axis_index("tensor")
    fac_b[:, :HALF] = fac_ref[:, columns(me)].astype(BF)
    fac_b[:, HALF:] = fac_ref[:, columns(1 - me)].astype(BF)

    def store(i):
        rows = pl.ds(i * STEP, STEP)
        return pltpu.make_async_copy(stage.at[rows], err_ref.at[rows], sems.at[i])

    for i in range(ROWS // STEP):
        rows = pl.ds(i * STEP, STEP)
        for n, (src, who) in enumerate(((own_ref, me), (other_ref, 1 - me))):
            approx = dot(basis_b_ref[:, rows], fac_b[:, n * HALF : (n + 1) * HALF], ((0,), (0,)))
            stage[rows, columns(who)] = (src[rows, :].astype(F32) - approx).astype(BF)
        store(i).start()
    for i in range(ROWS // STEP):
        store(i).wait()
    fac_copy.wait()


def residue(terms, basis_b, own, other, scale):
    return call(
        functools.partial(residue_kernel, scale),
        "residue",
        [WHOLE] * 7,
        [pltpu.HBM((ROWS, WIDTH), BF), pltpu.HBM((RANK, WIDTH), F32)],
        [
            pltpu.VMEM((RANK, WIDTH), F32),
            pltpu.VMEM((RANK, WIDTH), BF),
            pltpu.VMEM((ROWS, WIDTH), BF),
            pltpu.SemaphoreType.DMA((ROWS // STEP,)),
            pltpu.SemaphoreType.DMA,
        ],
        mib=24,
        flops=2 * RANK * ROWS * WIDTH,
        bytes_accessed=2 * ROWS * WIDTH,
    )(*terms, basis_b, in_vmem(own), in_vmem(other))


def ring_pairs(axes, flip, cross):
    pairs = []
    for index in range(64):
        for core in range(2):
            there = index ^ (flip << (2 * axes[core]))
            pairs.append((index * 2 + core, there * 2 + (core ^ cross)))
    return pairs


FLIPS = (1, 3, 2)
STAGES = ((0, 1), (1, 2), (2, 0))
SWAP = [(0, 1), (1, 0)]


def stages(crosses):
    moved = 0
    for axes, cross in zip(STAGES, crosses):
        yield (axes[::-1] if moved else axes), cross
        moved ^= cross


def spread(x, stage):
    axes, cross = stage
    terms = [lax.ppermute(x, AXES, ring_pairs(axes, flip, cross)) for flip in FLIPS]
    return terms + [lax.ppermute(x, "tensor", SWAP) if cross else x]


def add4(terms):
    a, b, c, d = (t.astype(F32) for t in terms)
    return (a + b) + (c + d)


def add_kernel(a_ref, b_ref, c_ref, d_ref, work_ref, sum_ref, work_out_ref):
    sum_ref[...] = (a_ref[...] + b_ref[...]) + (c_ref[...] + d_ref[...])


def add_after(terms, work):
    return call(
        add_kernel,
        "add_terms",
        [WHOLE] * 4 + [pl.BlockSpec(memory_space=pl.ANY)],
        [pltpu.VMEM(terms[0].shape, F32), pltpu.VMEM(work.shape, work.dtype)],
        bytes_accessed=10**6,
        aliases={4: 1},
    )(*terms, in_vmem(work))


def body(acts, grad_out, old_error, old_factor, piece_order):
    other_factor = lax.ppermute(old_factor, "tensor", SWAP)
    left, own_err, err, acts, grad_out = load_part(piece_order, old_factor, old_error, acts, grad_out)
    keep, give = term_part(piece_order, old_factor, other_factor, left, acts, grad_out)
    part = keep + lax.ppermute(give, "tensor", SWAP)
    first, second, third = stages((1, 0, 1))
    terms = spread(part, first)
    part, send = add_after(terms, send_part(piece_order, part, err))
    other_err = lax.ppermute(send, "tensor", SWAP)
    terms = spread(part, second)
    part, own = add_after(terms, corrected_half(False, part, acts, grad_out, own_err))
    terms = spread(part, third)
    part, other = add_after(terms, corrected_half(True, part, acts, grad_out, other_err))
    inverse, sums, right = right_part(part, lax.ppermute(part, "tensor", SWAP), own, other)
    basis_t, basis_b = basis_part(inverse, sums)
    first, second, third = stages((1, 1, 0))
    for stage in (first, second):
        right = add4(spread(right, stage)).astype(BF)
    terms = spread(right, third)
    new_error, new_factor = residue(terms, basis_b, own, other, 1.0 / lax.axis_size("dp"))
    return (new_error, basis_t.T, new_factor)


def solution(mesh):
    return jax.shard_map(
        body,
        mesh=mesh,
        in_specs=(P("dp", None), P("dp", "tensor"), P("dp", "tensor"), P(None, "tensor"), P()),
        out_specs=(P("dp", "tensor"), P(), P(None, "tensor")),
        check_vma=False,
    )
```

```python
import functools

import jax
import jax.numpy as jnp
from jax import lax
from jax.experimental import pallas as pl
from jax.experimental.pallas import tpu as pltpu
from jax.sharding import PartitionSpec as P

BF, F32 = jnp.bfloat16, jnp.float32
ROWS, WIDTH, HALF, RANK, TOK = 2304, 2304, 1152, 32, 512
PIECE, QUARTER, LANES = 288, 4, 128
BIG, SMALL = 768, 256
HI = lax.Precision.HIGHEST
AXES = ("dp", "tensor")

WHOLE = pl.BlockSpec(memory_space=pltpu.VMEM)
SCALARS = pl.BlockSpec(memory_space=pltpu.SMEM)
FAR = pl.BlockSpec(memory_space=pltpu.HBM)


def dot(a, b, dims, precision=None):
    return lax.dot_general(a, b, (dims, ((), ())), precision=precision, preferred_element_type=F32)


def in_vmem(x):
    return pltpu.with_memory_space_constraint(x, pltpu.VMEM)


def in_hbm(x):
    return pltpu.with_memory_space_constraint(x, pltpu.HBM)


def call(kernel, name, in_specs, outs, scratch=(), mib=16, flops=0, bytes_accessed=0, aliases=None):
    return pl.pallas_call(
        kernel,
        in_specs=in_specs,
        out_specs=[FAR if o.memory_space == pltpu.HBM else WHOLE for o in outs],
        out_shape=outs,
        scratch_shapes=list(scratch),
        compiler_params=pltpu.CompilerParams(vmem_limit_bytes=mib * 2**20),
        cost_estimate=pl.CostEstimate(flops=flops, bytes_accessed=bytes_accessed, transcendentals=0),
        name=name,
        input_output_aliases=aliases or {},
    )


def columns(who):
    return pl.ds(pl.multiple_of(who * HALF, LANES), HALF)


def regroup(order_ref, src_ref, dst_ref, first, rows=None):
    if rows is None:
        rows = pl.ds(0, src_ref.shape[0])
    lane = lax.broadcasted_iota(jnp.int32, (rows.size, LANES), 1)
    carry = None
    for k in range(QUARTER):
        piece = order_ref[first + k]
        start = pl.multiple_of(((piece * 9) // 4) * LANES, LANES)
        window = src_ref[rows, pl.ds(start, 3 * LANES)]
        shift = 32 * k - 32 * (piece % 4)
        window = pltpu.roll(window, jnp.where(shift < 0, shift + 3 * LANES, shift), 1)
        tile = (PIECE * k) // LANES
        tiles = [window[:, i * LANES : (i + 1) * LANES] for i in range(3)]
        if k:
            tiles[0] = jnp.where(lane < 32 * k, carry, tiles[0])
        carry = tiles[2]
        for i in range(3 if k == QUARTER - 1 else 2):
            dst_ref[rows, (tile + i) * LANES : (tile + i + 1) * LANES] = tiles[i]


def rows_at(i, size):
    return pl.ds(pl.multiple_of(i * size, size), size)


def load_kernel(far_order, far_fac, far_err, far_acts, far_grad, left_ref, own_ref, err_ref, acts_ref, grad_ref, fac_own_ref, fac, order_ref, sems):
    chunks = ROWS // BIG

    def fetch(i):
        rows = rows_at(i, BIG)
        return pltpu.make_async_copy(far_err.at[rows], err_ref.at[rows], sems.at[i])

    others = [
        pltpu.make_async_copy(src, dst, sems.at[chunks + n])
        for n, (src, dst) in enumerate(((far_fac, fac), (far_order, order_ref), (far_grad, grad_ref), (far_acts, acts_ref)))
    ]
    others[0].start()
    others[1].start()
    for i in range(chunks):
        fetch(i).start()
    others[2].start()
    others[3].start()
    me = lax.axis_index("tensor")
    others[0].wait()
    others[1].wait()
    regroup(order_ref, fac, fac_own_ref, me * QUARTER)

    @pl.loop(0, chunks)
    def _(i):
        fetch(i).wait()
        rows = rows_at(i, BIG)
        left_ref[:, rows] = dot(err_ref[rows, :], fac[...], ((1,), (1,))).T
        regroup(order_ref, err_ref, own_ref, me * QUARTER, rows)

    others[2].wait()
    others[3].wait()


def load_part(order, old_factor, old_error, acts, grad_out):
    return call(
        load_kernel,
        "load_part",
        [FAR] * 5,
        [
            pltpu.VMEM((RANK, ROWS), F32),
            pltpu.VMEM((ROWS, HALF), BF),
            pltpu.VMEM((ROWS, WIDTH), BF),
            pltpu.VMEM((TOK, ROWS), BF),
            pltpu.VMEM((TOK, WIDTH), BF),
            pltpu.VMEM((RANK, HALF), BF),
        ],
        [
            pltpu.VMEM((RANK, WIDTH), BF),
            pltpu.SMEM((2 * QUARTER,), jnp.int32),
            pltpu.SemaphoreType.DMA((ROWS // BIG + 4,)),
        ],
        flops=2 * RANK * ROWS * WIDTH,
        bytes_accessed=2 * ROWS * WIDTH,
    )(in_hbm(order), in_hbm(old_factor), in_hbm(old_error), in_hbm(acts), in_hbm(grad_out))


def term_kernel(order_ref, fac_ref, other_ref, left_ref, acts_ref, grad_ref, keep_ref, give_ref, fac_new, total):
    me = lax.axis_index("tensor")
    fac_new[:, columns(me)] = fac_ref[...]
    regroup(order_ref, other_ref, fac_new.at[:, columns(1 - me)], me * QUARTER)
    u = dot(fac_new[...], grad_ref[...], ((1,), (1,)))
    high = u.astype(BF)
    low = (u - high.astype(F32)).astype(BF)
    both = dot(jnp.concatenate([high, low], 0), acts_ref[...], ((1,), (0,)))
    total[...] = left_ref[...] + (both[:RANK] + both[RANK:])
    half = RANK // 2
    keep_ref[...] = total[rows_at(me, half), :]
    give_ref[...] = total[rows_at(1 - me, half), :]


def term_part(order, old_factor, other_factor, left, acts, grad_out):
    half = pltpu.VMEM((RANK // 2, ROWS), F32)
    return call(
        term_kernel,
        "term_part",
        [SCALARS] + [WHOLE] * 5,
        [half, half],
        [pltpu.VMEM((RANK, WIDTH), BF), pltpu.VMEM((RANK, ROWS), F32)],
        flops=4 * RANK * ROWS * TOK,
        bytes_accessed=5 * 10**6,
    )(order, in_vmem(old_factor), other_factor, in_vmem(left), in_vmem(acts), in_vmem(grad_out))


def send_kernel(order_ref, after_ref, err_ref, send_ref):
    other = 1 - lax.axis_index("tensor")

    @pl.loop(0, ROWS // BIG)
    def _(i):
        regroup(order_ref, err_ref, send_ref, other * QUARTER, rows_at(i, BIG))


def send_part(order, after, err):
    return call(
        send_kernel,
        "send_part",
        [SCALARS, pl.BlockSpec(memory_space=pl.ANY), WHOLE],
        [pltpu.VMEM((ROWS, HALF), BF)],
        flops=10**9,
        bytes_accessed=4 * 10**6,
    )(order, after, in_vmem(err))[0]


def add_grad(acts_ref, grad_ref, who, err_ref, out_ref):
    @pl.loop(0, ROWS // BIG)
    def _(i):
        rows = pl.ds(pl.multiple_of(i * BIG, BIG), BIG)
        grad = dot(acts_ref[:, rows], grad_ref[:, columns(who)], ((0,), (0,)))
        out_ref[rows, :] = (grad + err_ref[rows, :].astype(F32)).astype(BF)


def half_kernel(other, after_ref, acts_ref, grad_ref, err_ref, out_ref):
    me = lax.axis_index("tensor")
    add_grad(acts_ref, grad_ref, 1 - me if other else me, err_ref, out_ref)


def corrected_half(other, after, acts, grad_out, err):
    return call(
        functools.partial(half_kernel, other),
        "corrected_other" if other else "corrected_own",
        [pl.BlockSpec(memory_space=pl.ANY)] + [WHOLE] * 3,
        [pltpu.VMEM((ROWS, HALF), BF)],
        flops=2 * TOK * ROWS * HALF,
        bytes_accessed=8 * 10**6,
    )(after, in_vmem(acts), in_vmem(grad_out), in_vmem(err))[0]


def split3(x):
    terms = []
    for _ in range(3):
        terms.append(x.astype(BF))
        x = x - terms[-1].astype(F32)
    return jnp.concatenate(terms, 0)


def inverse_factor(gram):
    row = lax.broadcasted_iota(jnp.int32, (RANK, RANK), 0)
    col = lax.broadcasted_iota(jnp.int32, (RANK, RANK), 1)
    work = jnp.concatenate([gram, (row == col).astype(F32)], 1)
    wide = lax.broadcasted_iota(jnp.int32, work.shape, 0)
    for k in range(0, RANK, 2):
        first = jnp.broadcast_to(work[:, k : k + 1], work.shape)
        second = jnp.broadcast_to(work[:, k + 1 : k + 2], work.shape)
        row0 = work[k : k + 1, :]
        inv0 = 1.0 / first[k : k + 1, :]
        ratio = first[k + 1 : k + 2, :] * inv0
        row1 = work[k + 1 : k + 2, :] - ratio * row0
        pivot1 = second[k + 1 : k + 2, :] - ratio * first[k + 1 : k + 2, :]
        second = second - first * ratio
        below = work - first * (row0 * inv0) - second * (row1 * (1.0 / pivot1))
        work = jnp.where(wide > k + 1, below, jnp.where(wide == k + 1, row1, work))
    pivots = jnp.sum(jnp.where(row == col, work[:, :RANK], 0.0), 1, keepdims=True)
    return work[:, RANK:] * lax.rsqrt(pivots)


def dot3(terms, b):
    n = terms.shape[0] // 3
    x = dot(terms, b, ((1,), (0,)))
    return x[:n] + (x[n : 2 * n] + x[2 * n :])


def dot6(a, b):
    n = a.shape[0]
    terms = split3(a)
    parts = []
    for drop in range(3):
        part = b.astype(BF)
        b = b - part.astype(F32)
        x = dot(terms[: (3 - drop) * n], part, ((1,), (0,)))
        parts.append([x[i * n : (i + 1) * n] for i in range(3 - drop)])
    (x11, x21, x31), (x12, x22), (x13,) = parts
    return x11 + ((x21 + x12) + (x31 + (x22 + x13)))


def right_kernel(keep_ref, took_ref, own_ref, other_ref, inverse_ref, sums_ref, right_ref):
    me = lax.axis_index("tensor")
    keep, took = keep_ref[...], took_ref[...]
    sums = jnp.concatenate([jnp.where(me == 0, keep, took), jnp.where(me == 0, took, keep)], 0)
    sums_ref[...] = sums
    terms = split3(sums)
    pairs = dot(terms, terms, ((1,), (1,)))
    blocks = [[pairs[i * RANK : (i + 1) * RANK, j * RANK : (j + 1) * RANK] for j in range(3)] for i in range(3)]
    gram = blocks[0][0] + ((blocks[0][1] + blocks[1][0]) + (blocks[1][1] + (blocks[0][2] + blocks[2][0])))
    halves = [dot3(terms, ref[...]) for ref in (own_ref, other_ref)]
    inverse = inverse_factor(gram)
    inverse_ref[...] = inverse
    for half, who in zip(halves, (me, 1 - me)):
        right_ref[:, columns(who)] = dot6(inverse, half).astype(BF)


def right_part(keep, took, own, other):
    return call(
        right_kernel,
        "right_part",
        [WHOLE] * 4,
        [pltpu.VMEM((RANK, RANK), F32), pltpu.VMEM((RANK, ROWS), F32), pltpu.VMEM((RANK, WIDTH), BF)],
        flops=2 * RANK * ROWS * WIDTH,
        bytes_accessed=2 * ROWS * WIDTH,
    )(keep, took, in_vmem(own), in_vmem(other))


def basis_kernel(inverse_ref, sums_ref, basis_ref, basis_b_ref):
    basis = dot(inverse_ref[...], sums_ref[...], ((1,), (0,)), HI)
    basis_ref[...] = basis
    basis_b_ref[...] = basis.astype(BF)


def basis_part(inverse, sums):
    return call(
        basis_kernel,
        "basis_part",
        [WHOLE] * 2,
        [pltpu.VMEM((RANK, ROWS), F32), pltpu.VMEM((RANK, ROWS), BF)],
        flops=12 * RANK * RANK * ROWS,
        bytes_accessed=10**6,
    )(in_vmem(inverse), in_vmem(sums))


STEP = 192


def residue_kernel(scale, a_ref, b_ref, c_ref, d_ref, basis_b_ref, own_ref, other_ref, err_ref, far_ref, fac_ref, fac_b, stage, sems, fac_sem):
    total = (a_ref[...].astype(F32) + b_ref[...].astype(F32)) + (c_ref[...].astype(F32) + d_ref[...].astype(F32))
    factor = total * scale
    fac_ref[...] = factor
    fac_copy = pltpu.make_async_copy(fac_ref, far_ref, fac_sem)
    fac_copy.start()
    me = lax.axis_index("tensor")
    fac_b[:, :HALF] = fac_ref[:, columns(me)].astype(BF)
    fac_b[:, HALF:] = fac_ref[:, columns(1 - me)].astype(BF)

    def store(i):
        rows = pl.ds(i * STEP, STEP)
        return pltpu.make_async_copy(stage.at[rows], err_ref.at[rows], sems.at[i])

    for i in range(ROWS // STEP):
        rows = pl.ds(i * STEP, STEP)
        for n, (src, who) in enumerate(((own_ref, me), (other_ref, 1 - me))):
            approx = dot(basis_b_ref[:, rows], fac_b[:, n * HALF : (n + 1) * HALF], ((0,), (0,)))
            stage[rows, columns(who)] = (src[rows, :].astype(F32) - approx).astype(BF)
        store(i).start()
    for i in range(ROWS // STEP):
        store(i).wait()
    fac_copy.wait()


def residue(terms, basis_b, own, other, scale):
    return call(
        functools.partial(residue_kernel, scale),
        "residue",
        [WHOLE] * 7,
        [pltpu.HBM((ROWS, WIDTH), BF), pltpu.HBM((RANK, WIDTH), F32)],
        [
            pltpu.VMEM((RANK, WIDTH), F32),
            pltpu.VMEM((RANK, WIDTH), BF),
            pltpu.VMEM((ROWS, WIDTH), BF),
            pltpu.SemaphoreType.DMA((ROWS // STEP,)),
            pltpu.SemaphoreType.DMA,
        ],
        mib=24,
        flops=2 * RANK * ROWS * WIDTH,
        bytes_accessed=2 * ROWS * WIDTH,
    )(*terms, basis_b, in_vmem(own), in_vmem(other))


def ring_pairs(axes, flip, cross):
    pairs = []
    for index in range(64):
        for core in range(2):
            there = index ^ (flip << (2 * axes[core]))
            pairs.append((index * 2 + core, there * 2 + (core ^ cross)))
    return pairs


FLIPS = (1, 3, 2)
STAGES = ((0, 1), (1, 2), (2, 0))
SWAP = [(0, 1), (1, 0)]


def stages(crosses):
    moved = 0
    for axes, cross in zip(STAGES, crosses):
        yield (axes[::-1] if moved else axes), cross
        moved ^= cross


def spread(x, stage):
    axes, cross = stage
    terms = [lax.ppermute(x, AXES, ring_pairs(axes, flip, cross)) for flip in FLIPS]
    return [lax.ppermute(x, "tensor", SWAP) if cross else x] + terms


def add4(terms):
    a, b, c, d = (t.astype(F32) for t in terms)
    return (a + b) + (c + d)


def add_kernel(a_ref, b_ref, c_ref, d_ref, work_ref, sum_ref, work_out_ref):
    sum_ref[...] = (a_ref[...] + b_ref[...]) + (c_ref[...] + d_ref[...])


def add_after(terms, work):
    return call(
        add_kernel,
        "add_terms",
        [WHOLE] * 4 + [pl.BlockSpec(memory_space=pl.ANY)],
        [pltpu.VMEM(terms[0].shape, F32), pltpu.VMEM(work.shape, work.dtype)],
        bytes_accessed=10**6,
        aliases={4: 1},
    )(*terms, in_vmem(work))


def body(acts, grad_out, old_error, old_factor, piece_order):
    other_factor = lax.ppermute(old_factor, "tensor", SWAP)
    left, own_err, err, acts, grad_out, own_factor = load_part(piece_order, old_factor, old_error, acts, grad_out)
    keep, give = term_part(piece_order, own_factor, other_factor, left, acts, grad_out)
    part = keep + lax.ppermute(give, "tensor", SWAP)
    first, second, third = stages((1, 0, 1))
    terms = spread(part, first)
    part, send = add_after(terms, send_part(piece_order, part, err))
    other_err = lax.ppermute(send, "tensor", SWAP)
    terms = spread(part, second)
    part, own = add_after(terms, corrected_half(False, part, acts, grad_out, own_err))
    terms = spread(part, third)
    part, other = add_after(terms, corrected_half(True, part, acts, grad_out, other_err))
    inverse, sums, right = right_part(part, lax.ppermute(part, "tensor", SWAP), own, other)
    basis_t, basis_b = basis_part(inverse, sums)
    first, second, third = stages((1, 1, 0))
    for stage in (first, second):
        right = add4(spread(right, stage)).astype(BF)
    terms = spread(right, third)
    new_error, new_factor = residue(terms, basis_b, own, other, 1.0 / lax.axis_size("dp"))
    return (new_error, basis_t.T, new_factor)


def solution(mesh):
    return jax.shard_map(
        body,
        mesh=mesh,
        in_specs=(P("dp", None), P("dp", "tensor"), P("dp", "tensor"), P(None, "tensor"), P()),
        out_specs=(P("dp", "tensor"), P(), P(None, "tensor")),
        check_vma=False,
    )
```
